128 devices in a mesh: row: 8 (over z, y_hi), col: 16 (over x, y_lo, core).
Axes of the slice: x: 4, y: 4 (y_hi: 2, y_lo: 2; y = y_hi * 2 + y_lo), z: 4, core: 2. Of those that a mesh axis runs over, the one named last changes fastest.
Arguments:
- context_frames: bfloat16 [4, 768, 4096], P(None, 'row', 'col'), may hold values from -6 to 6
- latent_noise: bfloat16 [48, 256, 8], P('row', 'col'), may hold values from -6 to 6
- latent_proj: bfloat16 [8, 384], replicated, may hold values from -2 to 2
- coarse_context: bfloat16 [1024, 384], replicated, may hold values from -0.1875 to 0.1875
- fine_context: bfloat16 [256, 192], replicated, may hold values from -0.375 to 0.375
- coarse_gates: bfloat16 [6912, 768], replicated, may hold values from -0.078125 to 0.078125
- coarse_candidate: bfloat16 [6912, 384], replicated, may hold values from -0.078125 to 0.078125
- fine_gates: bfloat16 [3456, 384], replicated, may hold values from -0.109375 to 0.109375
- fine_candidate: bfloat16 [3456, 192], replicated, may hold values from -0.109375 to 0.109375
- upsample_proj: bfloat16 [384, 768], replicated, may hold values from -0.3125 to 0.3125
- head_proj: bfloat16 [192, 64], replicated, may hold values from -0.4375 to 0.4375
Outputs:
- forecast: float32 [2, 768, 4096], P(None, 'row', 'col')
The draws below stay inside these ranges and needn't reach their ends.
All inputs are finite; a program needn't handle non-finite values.
Results may differ from the reference program's by a relative error of at most 0.0055.
Values may be sent and summed in bfloat16 or wider, within the bound.
No kernel may reach another device: no remote copies, remote signals or barrier semaphores. Data moves between devices by JAX's collectives and lax.ppermute only.
A program may use at most 128 MiB of HBM per device.

```python
import jax
import jax.numpy as jnp

C2 = 384
C1 = 192
LAT = 8
FRAMES = 4
STEPS = 2
ROWS2 = 48
COLS2 = 256
PIX_ROWS = 768
PIX_COLS = 4096


def steps_of(stream_key, extent, split, smallest, high):
    level = 1.0
    for position, shards_of in split:
        heights = jax.random.uniform(jax.random.fold_in(jax.random.fold_in(stream_key, 6), position), (shards_of,), jnp.float32, smallest / len(split), high / len(split))
        level = level * jnp.repeat(jnp.exp(heights), extent[position] // shards_of).reshape((-1,) + (1,) * (len(extent) - 1 - position))
    return level


def noise(key, extent, width, limit, pieces=(), dtype=jnp.bfloat16):
    array = width * jax.random.normal(key, extent, jnp.float32)
    if pieces:
        array = array * steps_of(key, extent, pieces, -0.22, 0.18)
    return jnp.clip(array, -limit, limit).astype(dtype)


def setup_inputs(seed: int = 0) -> dict:
    key_of = jax.random.split(jax.random.key(seed), 12)
    return {
        "context_frames": noise(key_of[0], (FRAMES, PIX_ROWS, PIX_COLS), 1.0, 6.0, ((1, 8), (2, 16))),
        "latent_noise": noise(key_of[1], (ROWS2, COLS2, LAT), 1.0, 6.0, ((0, 8), (1, 16))),
        "latent_proj": noise(key_of[2], (LAT, C2), LAT ** -0.5, 2.0),
        "coarse_context": noise(key_of[3], (FRAMES * 256, C2), (FRAMES * 256) ** -0.5, 0.1875),
        "fine_context": noise(key_of[4], (FRAMES * 64, C1), (FRAMES * 64) ** -0.5, 0.375),
        "coarse_gates": noise(key_of[5], (18 * C2, 2 * C2), (18 * C2) ** -0.5, 0.078125),
        "coarse_candidate": noise(key_of[6], (18 * C2, C2), (18 * C2) ** -0.5, 0.078125),
        "fine_gates": noise(key_of[7], (18 * C1, 2 * C1), (18 * C1) ** -0.5, 0.109375),
        "fine_candidate": noise(key_of[8], (18 * C1, C1), (18 * C1) ** -0.5, 0.109375),
        "upsample_proj": noise(key_of[9], (C2, 4 * C1), C2 ** -0.5, 0.3125),
        "head_proj": noise(key_of[10], (C1, 64), C1 ** -0.5, 0.4375),
    }


def to_depth(frames, factor):
    count, height, breadth = frames.shape
    blocks = frames.reshape(count, height // factor, factor, breadth // factor, factor)
    return blocks.transpose(1, 3, 0, 2, 4).reshape(height // factor, breadth // factor, count * factor * factor)


def to_space(value, factor):
    height, breadth, total = value.shape
    channels = total // (factor * factor)
    blocks = value.reshape(height, breadth, factor, factor, channels)
    return blocks.transpose(0, 2, 1, 3, 4).reshape(height * factor, breadth * factor, channels)


def project(value, weight):
    flat = value.reshape(-1, value.shape[-1])
    result = jnp.dot(flat, weight, preferred_element_type=jnp.float32)
    return result.reshape(value.shape[:-1] + (weight.shape[1],))


def conv_same(value, weight):
    height, breadth, channels = value.shape
    padded = jnp.pad(value, ((1, 1), (1, 1), (0, 0)))
    total = jnp.zeros((height * breadth, weight.shape[1]), jnp.float32)
    for kernel_tap in range(9):
        shift_row = kernel_tap // 3
        shift_col = kernel_tap % 3
        piece = padded[shift_row:shift_row + height, shift_col:shift_col + breadth].reshape(height * breadth, channels)
        total = total + jnp.dot(piece, weight[kernel_tap * channels:(kernel_tap + 1) * channels], preferred_element_type=jnp.float32)
    return total.reshape(height, breadth, weight.shape[1])


def gru_step(inputs, state, gate_kernel, cand_kernel):
    channels = state.shape[-1]
    gates = conv_same(jnp.concatenate([inputs, state], -1), gate_kernel)
    reset = jax.nn.sigmoid(gates[..., :channels])
    update = jax.nn.sigmoid(gates[..., channels:])
    reset_state = (reset * state).astype(jnp.bfloat16)
    candidate = jnp.tanh(conv_same(jnp.concatenate([inputs, reset_state], -1), cand_kernel))
    return (update * state + (1.0 - update) * candidate).astype(jnp.bfloat16)


def reference(context_frames, latent_noise, latent_proj, coarse_context, fine_context, coarse_gates, coarse_candidate, fine_gates, fine_candidate, upsample_proj, head_proj):
    coarse_state = jnp.tanh(project(to_depth(context_frames, 16), coarse_context)).astype(jnp.bfloat16)
    fine_state = jnp.tanh(project(to_depth(context_frames, 8), fine_context)).astype(jnp.bfloat16)
    coarse_input = project(latent_noise, latent_proj).astype(jnp.bfloat16)
    outputs = []
    for step_index in range(STEPS):
        coarse_state = gru_step(coarse_input, coarse_state, coarse_gates, coarse_candidate)
        fine_input = to_space(project(coarse_state, upsample_proj), 2).astype(jnp.bfloat16)
        fine_state = gru_step(fine_input, fine_state, fine_gates, fine_candidate)
        outputs.append(to_space(project(fine_state, head_proj), 8)[..., 0])
    return jnp.stack(outputs, 0)
```

```python
import functools

import jax
import jax.numpy as jnp
from jax import lax
from jax.experimental import pallas as pl
from jax.experimental.pallas import tpu as pltpu
from jax.sharding import PartitionSpec as P

F32 = jnp.float32
BF16 = jnp.bfloat16

C2, C1 = 384, 192
GRID_ROWS, GRID_COLS = 48, 256
RC, CC = 6, 16
RF, CF = 12, 32
HC, HF = 5, 4
EC, EF = RC + 2 * HC, RF + 2 * HF
PC, PF = 32, 48
QC, QF = 24, 40
ROW_BUF, COL_BUF = 160, 144
TAPS = 9
KC = TAPS * C2 + 128

VMEM = pl.BlockSpec(memory_space=pltpu.VMEM)
SMEM = pl.BlockSpec(memory_space=pltpu.SMEM)
ANY = pl.BlockSpec(memory_space=pl.ANY)
HBM = pl.BlockSpec(memory_space=pltpu.HBM)


def dot(a, b):
    return jnp.dot(a, b, preferred_element_type=F32)


def dot_t(a, b):
    return lax.dot_general(a, b, (((1,), (1,)), ((), ())), preferred_element_type=F32)


def sigmoid(x):
    return 0.5 * jnp.tanh(0.5 * x) + 0.5


def iota(shape, dim):
    return lax.broadcasted_iota(jnp.int32, shape, dim)


def tiles_get(ref, rows):
    return jnp.concatenate([ref[t, rows, :] for t in range(ref.shape[0])], 1)


def tiles_put(ref, rows, value):
    lanes = ref.shape[0] * 128
    if value.shape[1] < lanes:
        value = jnp.concatenate([value, jnp.zeros((value.shape[0], lanes - value.shape[1]), F32)], 1)
    for t in range(ref.shape[0]):
        ref[t, rows, :] = value[:, 128 * t : 128 * t + 128]


def indicator(cond):
    return jnp.where(cond, 1.0, 0.0).astype(BF16)


def start_kernel(
    place,
    frames_hbm,
    noise_hbm,
    context2_hbm,
    context1_hbm,
    hc_out,
    hf_out,
    noise_out,
    even_out,
    odd_out,
    frames,
    noise,
    context2,
    context1,
    buf,
    sem,
):
    moves = [
        pltpu.make_async_copy(src, dst, sem.at[i])
        for i, (src, dst) in enumerate(
            ((frames_hbm, frames), (context2_hbm, context2), (context1_hbm, context1), (noise_hbm, noise))
        )
    ]
    for copy in moves:
        copy.start()

    def pick(shift, parity):
        row, col = iota((128, 256), 0), iota((128, 256), 1)
        count = 256 >> shift
        j = 2 * (row >> (8 - shift)) + parity
        return indicator(col == ((row & (count - 1)) << shift) + j)

    moves[0].wait()
    zeros = jnp.zeros((64, 256), BF16)
    even, odd = [], []
    for r in range(RC):
        band = frames[:, 16 * r : 16 * r + 16, :].reshape(64, 256)
        even += [band, zeros]
        odd += [zeros, band]
    even, odd = jnp.concatenate(even, 0), jnp.concatenate(odd, 0)

    def turned(shift):
        both = dot_t(pick(shift, 0), even) + dot_t(pick(shift, 1), odd)
        return both.astype(BF16)

    deep = turned(4)
    left = jnp.concatenate(
        [
            jnp.concatenate([deep[16 * j : 16 * j + 16, 128 * r : 128 * r + 128] for r in range(RC)], 0)
            for j in range(8)
        ],
        1,
    )
    row, col = iota((256, 256), 0), iota((256, 256), 1)
    swap = indicator(col == ((row & 15) << 4) + (row >> 4))
    moves[1].wait()
    moved = [dot(swap, context2[256 * f : 256 * f + 256, :]).astype(BF16) for f in range(4)]
    weight = jnp.concatenate([moved[f][16 * j : 16 * j + 16] for j in range(16) for f in range(4)], 0)
    state2 = jnp.tanh(dot(left, weight))
    hc_out[...] = state2.astype(BF16).reshape(RC, CC, C2)

    deep = turned(3)
    left = jnp.concatenate(
        [
            jnp.concatenate([deep[32 * j : 32 * j + 32, 128 * r : 128 * r + 128] for r in range(RC)], 0)
            for j in range(4)
        ],
        1,
    )
    row, col = iota((512, 256), 0), iota((512, 256), 1)
    moves[2].wait()
    source = (((row >> 4) & 3) << 6) + ((row & 7) << 3) + (row >> 6)
    for q in range(2):
        spread = indicator((col == source) & (((row >> 3) & 1) == q))
        weight = dot_t(spread, context1[...]).astype(BF16)
        state1 = jnp.tanh(dot(left, weight)).astype(BF16)
        for r in range(RC):
            hf_out[2 * r + q] = state1[CF * r : CF * r + CF]

    moves[3].wait()
    diagonal = indicator(iota((16, 16), 0) == iota((16, 16), 1))
    turned_noise = dot_t(diagonal, noise[...].reshape(RC * 8, CC))
    turned_noise = jnp.concatenate([turned_noise, jnp.zeros((16, 128 - 8 * RC), F32)], 1)
    noise_out[...] = turned_noise.astype(BF16)
    low_noise = pltpu.roll(turned_noise, 128 - 8 * (RC - HC), 1)

    up_first = (place[0] & 1) == 1
    for target, up in ((even_out, up_first), (odd_out, jnp.logical_not(up_first))):
        c_top = state2[: HC * CC]
        c_low = state2[(RC - HC) * CC :]
        buf[0:80, :] = jnp.where(up, c_top, c_low)
        for half in range(2):
            f_top = hf_out[2 * half : 2 * half + 2].reshape(64, C1).astype(F32)
            f_low = hf_out[RF - HF + 2 * half : RF - HF + 2 * half + 2].reshape(64, C1).astype(F32)
            buf[80:144, C1 * half : C1 * half + C1] = jnp.where(up, f_top, f_low)
        buf[144:160, :] = jnp.zeros((16, C2), F32)
        buf[144:160, 0:128] = jnp.where(up, turned_noise, low_noise)
        target[...] = buf[...].astype(BF16)


def column_kernel(
    place, hc, hf, noise, even_in, odd_in, after, ec_out, ef_out, en_out, even_out, odd_out, sc, sf, sn, buf
):
    up_first = (place[0] & 1) == 1
    above = jnp.where(up_first, even_in[...].astype(F32), odd_in[...].astype(F32))
    below = jnp.where(up_first, odd_in[...].astype(F32), even_in[...].astype(F32))
    tiles_put(sc, pl.ds(0, 80), above[0:80])
    tiles_put(sc, pl.ds(80, 96), hc[...].reshape(RC * CC, C2).astype(F32))
    tiles_put(sc, pl.ds(176, 80), below[0:80])
    for half in range(2):
        tiles_put(sf, pl.ds(64 * half, 64), above[80:144, C1 * half : C1 * half + C1])
        tiles_put(sf, pl.ds(512 + 64 * half, 64), below[80:144, C1 * half : C1 * half + C1])
    tiles_put(sf, pl.ds(128, 384), hf[...].reshape(RF * CF, C1).astype(F32))
    tiles_put(sf, pl.ds(640, 128), jnp.zeros((128, C1), F32))
    sn[...] = jnp.zeros(sn.shape, F32)
    for h in range(HC):
        sn[16 * h : 16 * h + 16, 0:8] = above[144:160, 8 * h : 8 * h + 8]
        sn[16 * (HC + RC + h) : 16 * (HC + RC + h) + 16, 0:8] = below[144:160, 8 * h : 8 * h + 8]
    for h in range(RC):
        sn[16 * (HC + h) : 16 * (HC + h) + 16, 0:8] = noise[:, 8 * h : 8 * h + 8].astype(F32)

    ec_out[...] = tiles_get(sc, pl.ds(0, EC * CC)).astype(BF16).reshape(EC, CC, C2)
    ef_out[...] = tiles_get(sf, pl.ds(0, EF * CF))[:, :C1].astype(BF16).reshape(EF, CF, C1)
    en_out[...] = sn[...].astype(BF16).reshape(EC, CC, 128)

    left_first = (place[1] & 1) == 1
    for target, left in ((even_out, left_first), (odd_out, jnp.logical_not(left_first))):
        c_from = jnp.where(left, 0, CC - HC)
        f_from = jnp.where(left, 0, CF - HF)
        buf[128:144, :] = jnp.zeros((16, C2), F32)
        for k in range(HC):
            buf[16 * k : 16 * k + 16, :] = tiles_get(sc, pl.ds(c_from + k, 16, stride=CC))
            strip = sn[pl.ds(c_from + k, 16, stride=CC), :]
            buf[128:144, 8 * k : 8 * k + 8] = strip[:, 0:8]
        for k in range(HF):
            at, lane = 80 + 24 * (k % 2), C1 * (k // 2)
            buf[at : at + 24, lane : lane + C1] = tiles_get(sf, pl.ds(f_from + k, 24, stride=CF))[:, :C1]
        target[...] = buf[...].astype(BF16)


def coarse_weights_kernel(
    proj_hbm, gates_hbm, cand_hbm, wg_out, wc_out, token, proj, gates, cand, acc_g, acc_c, sem
):
    count = [0]

    def move(src, dst):
        copy = pltpu.make_async_copy(src, dst, sem.at[count[0]])
        count[0] += 1
        copy.start()
        return copy

    first = move(proj_hbm, proj)
    inputs, states = [], []
    for hbm, held in ((gates_hbm, gates), (cand_hbm, cand)):
        inputs.append([move(hbm.at[pl.ds(2 * C2 * t, C2), :], held.at[t]) for t in range(TAPS)])
    for hbm, target in ((gates_hbm, wg_out), (cand_hbm, wc_out)):
        for t in range(TAPS):
            states.append(move(hbm.at[pl.ds(2 * C2 * t + C2, C2), :], target.at[pl.ds(C2 * t, C2), :]))
    acc_g[...] = jnp.zeros(acc_g.shape, F32)
    acc_c[...] = jnp.zeros(acc_c.shape, F32)
    first.wait()
    token[...] = jnp.zeros(token.shape, F32)
    wide = jnp.concatenate([proj[...].astype(F32), jnp.zeros((8, C2), F32)], 0).astype(BF16)
    for copies, held, acc in ((inputs[0], gates, acc_g), (inputs[1], cand, acc_c)):
        for t in range(TAPS):
            copies[t].wait()
            acc[8 * t : 8 * t + 8, :] = dot(wide, held[t])[0:8]
    wg_out[TAPS * C2 :, :] = acc_g[...].astype(BF16)
    wc_out[TAPS * C2 :, :] = acc_c[...].astype(BF16)
    for copy in states:
        copy.wait()


def fine_weights_kernel(
    after, gates_hbm, cand_hbm, up_hbm, head_hbm, wg_out, wc_out, up_out, head_out, up, head, sem
):
    moves = [
        pltpu.make_async_copy(src, dst, sem.at[i])
        for i, (src, dst) in enumerate(
            ((up_hbm, up), (head_hbm, head), (gates_hbm, wg_out), (cand_hbm, wc_out))
        )
    ]
    for copy in moves:
        copy.start()
    moves[1].wait()
    row, col = iota((2048, 64), 0), iota((2048, 64), 1)
    spread = indicator(col == ((row >> 8) << 3) + (row & 7))
    head_out[...] = dot(spread, head[...]).astype(BF16)
    moves[0].wait()
    wide = up[...].astype(F32)
    zeros = jnp.zeros((C2, 256 - C1), F32)
    for i in range(4):
        part = jnp.concatenate([wide[:, C1 * i : C1 * i + C1], zeros], 1)
        up_out[:, 256 * i : 256 * i + 256] = part.astype(BF16)
    moves[2].wait()
    moves[3].wait()


def main_kernel(
    place,
    ec,
    ef,
    en,
    even_in,
    odd_in,
    wg2,
    wc2,
    wg1,
    wc1,
    wup,
    whead,
    out,
    sc,
    sf,
    xf,
    hf,
    sn,
    patch,
    gate_u,
    reset_h,
    next_h,
    gate_uf,
    copies,
    frame,
):
    row0, col0 = place[0], place[1]
    left_first = (col0 & 1) == 1
    left = jnp.where(left_first, even_in[...].astype(F32), odd_in[...].astype(F32))
    right = jnp.where(left_first, odd_in[...].astype(F32), even_in[...].astype(F32))

    xf[...] = jnp.zeros(xf.shape, F32)
    hf[...] = jnp.zeros(hf.shape, F32)
    sn[...] = jnp.zeros(sn.shape, F32)
    patch[...] = jnp.zeros(patch.shape, F32)
    gate_u[...] = jnp.zeros(gate_u.shape, F32)
    reset_h[...] = jnp.zeros(reset_h.shape, F32)
    next_h[...] = jnp.zeros(next_h.shape, F32)
    gate_uf[...] = jnp.zeros(gate_uf.shape, F32)
    for h in range(EC):
        tiles_put(sc, pl.ds(PC * h + 8, CC), ec[h].astype(F32))
        sn[PC * h + 8 : PC * h + 24, :] = en[h].astype(F32)
    for k in range(HC):
        for side, at in ((left, 8 - HC + k), (right, 8 + CC + k)):
            tiles_put(sc, pl.ds(at, EC, stride=PC), side[16 * k : 16 * k + 16])
            strip = jnp.concatenate([side[128:144, 8 * k : 8 * k + 8], jnp.zeros((16, 120), F32)], 1)
            sn[pl.ds(at, EC, stride=PC), :] = strip
    for h in range(EF):
        tiles_put(hf, pl.ds(PF * h + 8, CF), ef[h].astype(F32))
    for k in range(HF):
        at, lane = 80 + 24 * (k % 2), C1 * (k // 2)
        for side, col in ((left, 8 - HF + k), (right, 8 + CF + k)):
            tiles_put(hf, pl.ds(col, EF, stride=PF), side[at : at + EF, lane : lane + C1])
    sf[:, C1 : 2 * C1] = tiles_get(hf, pl.ds(0, EF * PF))[:, :C1]

    noise = sn[...].reshape(EC, PC, 128)
    total = None
    for dx in range(3):
        part = None
        for dy in range(3):
            moved = noise[dy : dy + EC - 2]
            if dy or dx:
                moved = pltpu.roll(moved, 8 * (3 * dy + dx), 2)
            part = moved if part is None else part + moved
        part = part[:, 3 + dx : 3 + dx + QC, :]
        total = part if total is None else total + part
    patch[:, 0:QC, :] = total

    def spread(field, width, pitch, lanes, rows_out, narrow):
        for dx in range(3):
            moved = field(dx)
            rows = rows_out + 2
            copies[dx, 0 : rows * pitch, 0:lanes] = moved.reshape(rows * pitch, lanes).astype(BF16)
            if narrow:
                inner = moved[1 : 1 + rows_out].reshape(rows_out * pitch, lanes)
                copies[3 + dx, 0 : rows_out * pitch, 0:lanes] = inner.astype(BF16)
        parts = []
        for dy in range(3):
            for dx in range(3):
                if dy == 1 and narrow:
                    parts.append(copies[3 + dx, 0 : rows_out * pitch, 0:lanes])
                else:
                    parts.append(copies[dx, dy * pitch : (dy + rows_out) * pitch, 0:lanes])
        return parts

    def coarse_conv(field, rows_out, offset, weight):
        parts = spread(field, C2, QC, C2, rows_out, True)
        near = patch[offset : offset + rows_out, offset : offset + QC, :]
        parts.append(near.reshape(rows_out * QC, 128).astype(BF16))
        return dot(jnp.concatenate(parts, 1), weight[...])

    def inside(shape, row_from, row_end, col_from, col_end):
        row = iota(shape, 0) + row_from
        col = iota(shape, 1) + col_from
        return (row >= 0) & (row < row_end) & (col >= 0) & (col < col_end)

    def coarse_step(step, read):
        rows = 14 - 4 * step
        gates = coarse_conv(lambda dx: read(0, dx, rows + 2, QC), rows, 2 * step, wg2)
        reset_h[0:rows, 0:QC, :] = sigmoid(gates[:, :C2]).reshape(rows, QC, C2) * read(1, 1, rows, QC)
        gate_u[0:rows, 0:QC, :] = sigmoid(gates[:, C2:]).reshape(rows, QC, C2)
        cand = jnp.tanh(
            coarse_conv(lambda dx: reset_h[0:rows, dx : dx + QC, :], rows - 2, 2 * step + 1, wc2)
        ).reshape(rows - 2, QC, C2)
        update = gate_u[1 : rows - 1, 1 : 1 + QC, :]
        state = update * read(2, 2, rows - 2, QC) + (1.0 - update) * cand
        first = 2 + 2 * step
        valid = inside(state.shape, row0 * RC + first - HC, GRID_ROWS, col0 * CC + first - HC, GRID_COLS)
        return jnp.where(valid, state, 0.0).astype(BF16)

    def fine_input(state, rows, row_to, col_to):
        value = dot(state.reshape(rows * QC, C2), wup[...])
        for q in range(2):
            for p in range(2):
                lane = 256 * (2 * q + p)
                for r in range(rows):
                    at = (row_to + 2 * r + q) * PF + col_to + p
                    tiles_put(xf, pl.ds(at, QC, stride=2), value[QC * r : QC * r + QC, lane : lane + 256])
        sf[:, 0:C1] = tiles_get(xf, pl.ds(0, EF * PF))[:, :C1]

    def fine_step(step):
        rows = 18 - 4 * step
        first = 2 * step
        field = sf[...].reshape(EF, PF, 2 * C1)
        parts = spread(
            lambda dx: field[first : first + rows + 2, 4 + first + dx : 4 + first + dx + QF, :],
            2 * C1, QF, 2 * C1, rows, True,
        )
        gates = dot(jnp.concatenate(parts, 1), wg1[...])
        reset = sigmoid(gates[:, :C1]).reshape(rows, QF, C1)
        state = tiles_get(hf, pl.ds(0, EF * PF))[:, :C1].reshape(EF, PF, C1)
        near = reset * state[first + 1 : first + 1 + rows, 5 + first : 5 + first + QF, :]
        gate_uf[0:rows, 0:QF, :] = sigmoid(gates[:, C1:]).reshape(rows, QF, C1)
        for r in range(rows):
            at = (first + 1 + r) * PF + 5 + first
            sf[at : at + QF, C1 : 2 * C1] = near[r]
        field = sf[...].reshape(EF, PF, 2 * C1)
        width = CF if step else QF
        parts = spread(
            lambda dx: field[first + 1 : first + 1 + rows, 5 + first + dx : 5 + first + dx + width, :],
            2 * C1, width, 2 * C1, rows - 2, width % 16 != 0,
        )
        cand = jnp.tanh(dot_t(jnp.concatenate(parts, 1), wc1[...])).reshape(rows - 2, width, C1)
        update = gate_uf[1 : rows - 1, 1 : 1 + width, :]
        old = state[first + 2 : first + rows, 6 + first : 6 + first + width, :]
        new = update * old + (1.0 - update) * cand
        if step == 0:
            valid = inside(
                new.shape, row0 * RF + 2 - HF, 2 * GRID_ROWS, col0 * CF + 2 - HF, 2 * GRID_COLS
            )
            new = jnp.where(valid, new, 0.0).astype(BF16).astype(F32)
            for r in range(rows - 2):
                at = (2 + r) * PF + 6
                tiles_put(hf, pl.ds(at, QF), new[r])
                sf[at : at + QF, C1 : 2 * C1] = new[r]
            return new[2:14, 2 : 2 + CF, :].reshape(RF * CF, C1).astype(BF16)
        return new.reshape(RF * CF, C1).astype(BF16)

    def emit(step, state):
        mask = (iota((RF, CF, 256), 2) >> 3) == iota((RF, CF, 256), 1)
        for r in range(8):
            value = dot_t(state, whead[256 * r : 256 * r + 256, :]).reshape(RF, CF, 256)
            tiles_put(frame, pl.ds(r, RF, stride=8), jnp.sum(jnp.where(mask, value, 0.0), axis=1))
        out[step] = tiles_get(frame, pl.ds(0, 8 * RF))

    field2 = tiles_get(sc, pl.ds(0, EC * PC)).reshape(EC, PC, C2)
    state2 = coarse_step(0, lambda r, c, rows, cols: field2[r : r + rows, 3 + c : 3 + c + cols, :])
    next_h[:, 0:QC, :] = state2.astype(F32)
    fine_input(state2[1:11], 10, 0, 2)
    state1 = fine_step(0)
    emit(0, state1)
    state2 = coarse_step(1, lambda r, c, rows, cols: next_h[r : r + rows, c : c + cols, :])
    fine_input(state2, 8, 2, 6)
    emit(1, fine_step(1))


def in_hbm(value):
    return pltpu.with_memory_space_constraint(value, pltpu.HBM)


def swapped(value, axis, odd):
    pairs = []
    for i in range(odd, lax.axis_size(axis) - 1, 2):
        pairs += [(i, i + 1), (i + 1, i)]
    return lax.ppermute(value, axis, pairs)


def call(kernel, out_shape, in_specs, scratch, limit, flops, bytes_accessed, **extra):
    return pl.pallas_call(
        kernel,
        out_shape=out_shape,
        in_specs=in_specs,
        out_specs=[VMEM] * len(out_shape),
        scratch_shapes=scratch,
        compiler_params=pltpu.CompilerParams(vmem_limit_bytes=limit),
        cost_estimate=pl.CostEstimate(flops=flops, bytes_accessed=bytes_accessed, transcendentals=0),
        **extra,
    )


def on_device(
    context_frames,
    latent_noise,
    latent_proj,
    coarse_context,
    fine_context,
    coarse_gates,
    coarse_candidate,
    fine_gates,
    fine_candidate,
    upsample_proj,
    head_proj,
):
    place = jnp.stack([lax.axis_index("row"), lax.axis_index("col")]).astype(jnp.int32)
    shape = jax.ShapeDtypeStruct
    row_buf, col_buf = shape((ROW_BUF, C2), BF16), shape((COL_BUF, C2), BF16)

    hc, hf, noise, even, odd = call(
        start_kernel,
        [
            shape((RC, CC, C2), BF16),
            shape((RF, CF, C1), BF16),
            shape((16, 128), BF16),
            row_buf,
            row_buf,
        ],
        [SMEM] + [HBM] * 4,
        [
            pltpu.VMEM((4, 16 * RC, 16 * CC), BF16),
            pltpu.VMEM((RC, 8, CC), BF16),
            pltpu.VMEM((1024, C2), BF16),
            pltpu.VMEM((C1, 256), BF16),
            pltpu.VMEM((ROW_BUF, C2), F32),
            pltpu.SemaphoreType.DMA((4,)),
        ],
        16 << 20, 10**9, 2 << 20,
    )(
        place,
        in_hbm(context_frames),
        in_hbm(latent_noise.transpose(0, 2, 1)),
        in_hbm(coarse_context),
        in_hbm(fine_context.T),
    )

    even, odd = swapped(even, "row", 0), swapped(odd, "row", 1)

    wg2, wc2, token = call(
        coarse_weights_kernel,
        [shape((KC, 2 * C2), BF16), shape((KC, C2), BF16), shape((8, 128), F32)],
        [HBM] * 3,
        [
            pltpu.VMEM((8, C2), BF16),
            pltpu.VMEM((TAPS, C2, 2 * C2), BF16),
            pltpu.VMEM((TAPS, C2, C2), BF16),
            pltpu.VMEM((128, 2 * C2), F32),
            pltpu.VMEM((128, C2), F32),
            pltpu.SemaphoreType.DMA((4 * TAPS + 1,)),
        ],
        16 << 20, 10**9, 24 << 20,
    )(in_hbm(latent_proj), in_hbm(coarse_gates), in_hbm(coarse_candidate))

    ec, ef, en, even, odd = call(
        column_kernel,
        [
            shape((EC, CC, C2), BF16),
            shape((EF, CF, C1), BF16),
            shape((EC, CC, 128), BF16),
            col_buf,
            col_buf,
        ],
        [SMEM] + [VMEM] * 5 + [ANY],
        [
            pltpu.VMEM((3, EC * CC, 128), F32),
            pltpu.VMEM((2, 24 * CF, 128), F32),
            pltpu.VMEM((EC * CC, 128), F32),
            pltpu.VMEM((COL_BUF, C2), F32),
        ],
        8 << 20, 10**6, 2 << 20,
    )(place, hc, hf, noise, even, odd, token)

    even, odd = swapped(even, "col", 0), swapped(odd, "col", 1)

    wg1, wc1, up, head = call(
        fine_weights_kernel,
        [
            shape((18 * C1, 2 * C1), BF16),
            shape((C1, 18 * C1), BF16),
            shape((C2, 1024), BF16),
            shape((2048, C1), BF16),
        ],
        [ANY] + [HBM] * 4,
        [
            pltpu.VMEM((C2, 4 * C1), BF16),
            pltpu.VMEM((64, C1), BF16),
            pltpu.SemaphoreType.DMA((4,)),
        ],
        8 << 20, 10**8, 8 << 20,
    )(en, in_hbm(fine_gates), in_hbm(fine_candidate.T), in_hbm(upsample_proj), in_hbm(head_proj.T))

    (forecast,) = call(
        main_kernel,
        [shape((2, 96, 256), F32)],
        [SMEM] + [VMEM] * 11,
        [
            pltpu.VMEM((3, EC * PC, 128), F32),
            pltpu.VMEM((EF * PF, 2 * C1), F32),
            pltpu.VMEM((2, EF * PF + 16, 128), F32),
            pltpu.VMEM((2, EF * PF, 128), F32),
            pltpu.VMEM((EC * PC, 128), F32),
            pltpu.VMEM((EC - 2, PC, 128), F32),
            pltpu.VMEM((14, PC, C2), F32),
            pltpu.VMEM((14, PC, C2), F32),
            pltpu.VMEM((12, PC, C2), F32),
            pltpu.VMEM((18, PF, C1), F32),
            pltpu.VMEM((6, EF * QF, 2 * C1), BF16),
            pltpu.VMEM((2, 8 * RF, 128), F32),
        ],
        40 << 20, 9 * 10**9, 30 << 20,
    )(place, ec, ef, en, even, odd, wg2, wc2, wg1, wc1, up, head)
    return forecast


def solution(mesh):
    return jax.shard_map(
        on_device,
        mesh=mesh,
        in_specs=(
            P(None, "row", "col"),
            P("row", "col", None),
            P(),
            P(),
            P(),
            P(),
            P(),
            P(),
            P(),
            P(),
            P(),
        ),
        out_specs=P(None, "row", "col"),
        check_vma=False,
    )
```

```python
import functools

import jax
import jax.numpy as jnp
from jax import lax
from jax.experimental import pallas as pl
from jax.experimental.pallas import tpu as pltpu
from jax.sharding import PartitionSpec as P

F32 = jnp.float32
BF16 = jnp.bfloat16

C2, C1 = 384, 192
GRID_ROWS, GRID_COLS = 48, 256
RC, CC = 6, 16
RF, CF = 12, 32
HC, HF = 5, 4
EC, EF = RC + 2 * HC, RF + 2 * HF
PC = 32
QC, QF = 24, 40
PAD = 8
WF = 256
ROW_BUF, COL_BUF = 160, 144
TAPS = 9
KC = TAPS * C2 + 128

VMEM = pl.BlockSpec(memory_space=pltpu.VMEM)
SMEM = pl.BlockSpec(memory_space=pltpu.SMEM)
ANY = pl.BlockSpec(memory_space=pl.ANY)
HBM = pl.BlockSpec(memory_space=pltpu.HBM)


def dot(a, b):
    return jnp.dot(a, b, preferred_element_type=F32)


def dot_t(a, b):
    return lax.dot_general(a, b, (((1,), (1,)), ((), ())), preferred_element_type=F32)


def sigmoid(x):
    return 0.5 * jnp.tanh(0.5 * x) + 0.5


def iota(shape, dim):
    return lax.broadcasted_iota(jnp.int32, shape, dim)


def tiles_get(ref, rows):
    return jnp.concatenate([ref[t, rows, :] for t in range(ref.shape[0])], 1)


def pack_pair(a, b):
    return jnp.concatenate([a[:, 128:], b[:, 128:], a[:, :128] + pltpu.roll(b[:, :128], 64, 1)], 1)


def unpack_pair(both):
    mixed = both[:, 256:384]
    upper = iota(mixed.shape, 1) >= 64
    a = jnp.where(upper, mixed, 0.0)
    b = jnp.where(upper, pltpu.roll(mixed, 64, 1), 0.0)
    return jnp.concatenate([a, both[:, :128]], 1), jnp.concatenate([b, both[:, 128:256]], 1)


def tiles_put(ref, rows, value):
    lanes = ref.shape[0] * 128
    if value.shape[1] < lanes:
        value = jnp.concatenate([value, jnp.zeros((value.shape[0], lanes - value.shape[1]), F32)], 1)
    for t in range(ref.shape[0]):
        ref[t, rows, :] = value[:, 128 * t : 128 * t + 128]


def indicator(cond):
    return jnp.where(cond, 1.0, 0.0).astype(BF16)


def start_kernel(
    place,
    frames_hbm,
    noise_hbm,
    context2_hbm,
    context1_hbm,
    hc_out,
    hf_out,
    noise_out,
    even_out,
    odd_out,
    frames,
    noise,
    context2,
    context1,
    picks,
    swaps,
    spreads,
    buf,
    sem,
):
    moves = [
        pltpu.make_async_copy(src, dst, sem.at[i])
        for i, (src, dst) in enumerate(
            (
                (frames_hbm, frames),
                (context2_hbm, context2),
                (context1_hbm, context1.at[pl.ds(WF - C1, C1), :]),
                (noise_hbm, noise),
            )
        )
    ]
    for copy in moves:
        copy.start()

    def pick(shift, parity):
        row, col = iota((128, 256), 0), iota((128, 256), 1)
        count = 256 >> shift
        j = 2 * (row >> (8 - shift)) + parity
        return indicator(col == ((row & (count - 1)) << shift) + j)

    context1[0 : WF - C1, :] = jnp.zeros((WF - C1, 256), BF16)
    for shift in (4, 3):
        for parity in range(2):
            picks[4 - shift, parity] = pick(shift, parity)
    row, col = iota((256, 256), 0), iota((256, 256), 1)
    swaps[...] = indicator(col == ((row & 15) << 4) + (row >> 4))
    row, col = iota((512, 256), 0), iota((512, 256), 1)
    source = (((row >> 4) & 3) << 6) + ((row & 7) << 3) + (row >> 6)
    for q in range(2):
        spreads[q] = indicator((col == source) & (((row >> 3) & 1) == q))
    moves[0].wait()
    zeros = jnp.zeros((64, 256), BF16)
    even, odd = [], []
    for r in range(RC):
        band = frames[:, 16 * r : 16 * r + 16, :].reshape(64, 256)
        even += [band, zeros]
        odd += [zeros, band]
    even, odd = jnp.concatenate(even, 0), jnp.concatenate(odd, 0)

    def turned(shift):
        both = dot_t(picks[4 - shift, 0], even) + dot_t(picks[4 - shift, 1], odd)
        return both.astype(BF16)

    deep = turned(4)
    left = jnp.concatenate(
        [
            jnp.concatenate([deep[16 * j : 16 * j + 16, 128 * r : 128 * r + 128] for r in range(RC)], 0)
            for j in range(8)
        ],
        1,
    )
    moves[1].wait()
    swap = swaps[...]
    moved = [dot(swap, context2[256 * f : 256 * f + 256, :]).astype(BF16) for f in range(4)]
    weight = jnp.concatenate([moved[f][16 * j : 16 * j + 16] for j in range(16) for f in range(4)], 0)
    state2 = jnp.tanh(dot(left, weight))
    hc_out[...] = state2.astype(BF16).reshape(RC, CC, C2)

    deep = turned(3)
    left = jnp.concatenate(
        [
            jnp.concatenate([deep[32 * j : 32 * j + 32, 128 * r : 128 * r + 128] for r in range(RC)], 0)
            for j in range(4)
        ],
        1,
    )
    moves[2].wait()
    for q in range(2):
        weight = dot_t(spreads[q], context1[...]).astype(BF16)
        state1 = jnp.tanh(dot(left, weight)).astype(BF16)
        for r in range(RC):
            hf_out[2 * r + q] = state1[CF * r : CF * r + CF]

    moves[3].wait()
    diagonal = indicator(iota((16, 16), 0) == iota((16, 16), 1))
    turned_noise = dot_t(diagonal, noise[...].reshape(RC * 8, CC))
    turned_noise = jnp.concatenate([turned_noise, jnp.zeros((16, 128 - 8 * RC), F32)], 1)
    noise_out[...] = turned_noise.astype(BF16)
    low_noise = pltpu.roll(turned_noise, 128 - 8 * (RC - HC), 1)

    up_first = (place[0] & 1) == 1
    for target, up in ((even_out, up_first), (odd_out, jnp.logical_not(up_first))):
        c_top = state2[: HC * CC]
        c_low = state2[(RC - HC) * CC :]
        buf[0:80, :] = jnp.where(up, c_top, c_low)
        top = [hf_out[r : r + 2].reshape(64, WF).astype(F32) for r in (0, 2)]
        low = [hf_out[r : r + 2].reshape(64, WF).astype(F32) for r in (RF - HF, RF - HF + 2)]
        buf[80:144, :] = jnp.where(up, pack_pair(*top), pack_pair(*low))
        buf[144:160, :] = jnp.zeros((16, C2), F32)
        buf[144:160, 0:128] = jnp.where(up, turned_noise, low_noise)
        target[...] = buf[...].astype(BF16)


def column_kernel(
    place, hc, hf, noise, even_in, odd_in, after, ec_out, ef_out, en_out, even_out, odd_out, sc, sf, sn, buf
):
    up_first = (place[0] & 1) == 1
    above = jnp.where(up_first, even_in[...].astype(F32), odd_in[...].astype(F32))
    below = jnp.where(up_first, odd_in[...].astype(F32), even_in[...].astype(F32))
    tiles_put(sc, pl.ds(0, 80), above[0:80])
    tiles_put(sc, pl.ds(80, 96), hc[...].reshape(RC * CC, C2).astype(F32))
    tiles_put(sc, pl.ds(176, 80), below[0:80])
    for half, strip in enumerate(unpack_pair(above[80:144])):
        tiles_put(sf, pl.ds(64 * half, 64), strip)
    for half, strip in enumerate(unpack_pair(below[80:144])):
        tiles_put(sf, pl.ds(512 + 64 * half, 64), strip)
    tiles_put(sf, pl.ds(128, 384), hf[...].reshape(RF * CF, WF).astype(F32))
    tiles_put(sf, pl.ds(640, 128), jnp.zeros((128, WF), F32))
    sn[...] = jnp.zeros(sn.shape, F32)
    for h in range(HC):
        sn[16 * h : 16 * h + 16, 0:8] = above[144:160, 8 * h : 8 * h + 8]
        sn[16 * (HC + RC + h) : 16 * (HC + RC + h) + 16, 0:8] = below[144:160, 8 * h : 8 * h + 8]
    for h in range(RC):
        sn[16 * (HC + h) : 16 * (HC + h) + 16, 0:8] = noise[:, 8 * h : 8 * h + 8].astype(F32)

    ec_out[...] = tiles_get(sc, pl.ds(0, EC * CC)).astype(BF16).reshape(EC, CC, C2)
    ef_out[...] = tiles_get(sf, pl.ds(0, EF * CF)).astype(BF16).reshape(EF, CF, WF)
    en_out[...] = sn[...].astype(BF16).reshape(EC, CC, 128)

    left_first = (place[1] & 1) == 1
    for target, left in ((even_out, left_first), (odd_out, jnp.logical_not(left_first))):
        c_from = jnp.where(left, 0, CC - HC)
        f_from = jnp.where(left, 0, CF - HF)
        buf[128:144, :] = jnp.zeros((16, C2), F32)
        for k in range(HC):
            buf[16 * k : 16 * k + 16, :] = tiles_get(sc, pl.ds(c_from + k, 16, stride=CC))
            strip = sn[pl.ds(c_from + k, 16, stride=CC), :]
            buf[128:144, 8 * k : 8 * k + 8] = strip[:, 0:8]
        for k in range(2):
            strips = [tiles_get(sf, pl.ds(f_from + i, 24, stride=CF)) for i in (k, k + 2)]
            buf[80 + 24 * k : 104 + 24 * k, :] = pack_pair(*strips)
        target[...] = buf[...].astype(BF16)


def coarse_weights_kernel(
    proj_hbm, gates_hbm, cand_hbm, wg_out, wc_out, token, proj, gates, cand, acc_g, acc_c, sem
):
    count = [0]

    def move(src, dst):
        copy = pltpu.make_async_copy(src, dst, sem.at[count[0]])
        count[0] += 1
        copy.start()
        return copy

    first = move(proj_hbm, proj)
    inputs, states = [], []
    for hbm, held in ((gates_hbm, gates), (cand_hbm, cand)):
        inputs.append([move(hbm.at[pl.ds(2 * C2 * t, C2), :], held.at[t]) for t in range(TAPS)])
    for hbm, target in ((gates_hbm, wg_out), (cand_hbm, wc_out)):
        for t in range(TAPS):
            states.append(move(hbm.at[pl.ds(2 * C2 * t + C2, C2), :], target.at[pl.ds(C2 * t, C2), :]))
    acc_g[...] = jnp.zeros(acc_g.shape, F32)
    acc_c[...] = jnp.zeros(acc_c.shape, F32)
    first.wait()
    token[...] = jnp.zeros(token.shape, F32)
    wide = jnp.concatenate([proj[...].astype(F32), jnp.zeros((8, C2), F32)], 0).astype(BF16)
    for copies, held, acc in ((inputs[0], gates, acc_g), (inputs[1], cand, acc_c)):
        for t in range(TAPS):
            copies[t].wait()
            acc[8 * t : 8 * t + 8, :] = dot(wide, held[t])[0:8]
    wg_out[TAPS * C2 :, :] = acc_g[...].astype(BF16)
    wc_out[TAPS * C2 :, :] = acc_c[...].astype(BF16)
    for copy in states:
        copy.wait()


def fine_weights_kernel(
    after, gates_hbm, cand_hbm, up_hbm, head_hbm, wr_out, wu_out, wv_out, wc_out, up_out, head_out, gates, up, head, sem
):
    moves = [
        pltpu.make_async_copy(src, dst, sem.at[i])
        for i, (src, dst) in enumerate(
            (
                (up_hbm, up),
                (head_hbm, head),
                (gates_hbm, gates),
                (cand_hbm, wc_out.at[pl.ds(WF - C1, C1), :]),
            )
        )
    ]
    for copy in moves:
        copy.start()
    wc_out[0 : WF - C1, :] = jnp.zeros((WF - C1, 18 * C1), BF16)
    moves[1].wait()
    row, col = iota((1024, 64), 0), iota((1024, 64), 1)
    spread = indicator(col == ((row >> 7) << 3) + (row & 7))
    wide = jnp.concatenate([jnp.zeros((64, WF - C1), F32), head[...].astype(F32)], 1).astype(BF16)
    head_out[...] = dot(spread, wide).astype(BF16)
    moves[0].wait()
    wide = up[...].astype(F32)
    zeros = jnp.zeros((C2, 256 - C1), F32)
    for i in range(4):
        part = jnp.concatenate([wide[:, C1 * i : C1 * i + C1], zeros], 1)
        up_out[:, 256 * i : 256 * i + 256] = part.astype(BF16)
    moves[2].wait()
    for t in range(TAPS):
        rows = slice(2 * C1 * t, 2 * C1 * t + 2 * C1)
        part = gates[rows, 0:256].astype(F32)
        wr_out[rows, :] = jnp.concatenate([part[:, C1:256], part[:, :C1]], 1).astype(BF16)
        target, lane = (wv_out, 0) if t % 3 == 1 else (wu_out, 64 * (t % 3))
        target[2 * C1 * (t // 3) : 2 * C1 * (t // 3) + 2 * C1, lane : lane + 128] = gates[rows, 256:384]
    moves[3].wait()


def main_kernel(
    place,
    ec,
    ef,
    en,
    even_in,
    odd_in,
    wg2,
    wc2,
    wr1,
    wu1,
    wv1,
    wc1,
    wup,
    whead,
    out,
    first_h,
    sn,
    patch,
    reset_h,
    next_h,
    gate_u,
    fine_x,
    fine_h,
    fine_reset,
    fine_u,
    side_u,
    even_c,
    odd_c,
    even_f,
    odd_f,
    last_f,
):
    row0, col0 = place[0], place[1]
    left_first = (col0 & 1) == 1
    left = jnp.where(left_first, even_in[...].astype(F32), odd_in[...].astype(F32))
    right = jnp.where(left_first, odd_in[...].astype(F32), even_in[...].astype(F32))

    for ref, pitch, rows in (
        (reset_h, QC, EC), (next_h, QC, EC), (fine_x, QF, EF), (fine_h, QF, EF), (fine_reset, QF, EF)
    ):
        for t in range(ref.shape[0]):
            ref[t, 0 : PAD + 2 * pitch, :] = jnp.zeros((PAD + 2 * pitch, 128), F32)
            ref[t, PAD + (rows - 2) * pitch :, :] = jnp.zeros((2 * pitch + 8, 128), F32)
    sn[...] = jnp.zeros(sn.shape, F32)
    for h in range(EC):
        tiles_put(first_h, pl.ds(PC * h + 8, CC), ec[h].astype(F32))
        sn[PC * h + 8 : PC * h + 24, :] = en[h].astype(F32)
    for k in range(HC):
        for side, at in ((left, 8 - HC + k), (right, 8 + CC + k)):
            tiles_put(first_h, pl.ds(at, EC, stride=PC), side[16 * k : 16 * k + 16])
            strip = jnp.concatenate([side[128:144, 8 * k : 8 * k + 8], jnp.zeros((16, 120), F32)], 1)
            sn[pl.ds(at, EC, stride=PC), :] = strip
    for h in range(EF):
        tiles_put(fine_h, pl.ds(PAD + QF * h + HF, CF), ef[h].astype(F32))
    for side, col in ((left, 0), (right, HF + CF)):
        for k in range(2):
            for i, strip in enumerate(unpack_pair(side[80 + 24 * k : 80 + 24 * k + EF])):
                tiles_put(fine_h, pl.ds(PAD + col + k + 2 * i, EF, stride=QF), strip)

    noise = sn[...].reshape(EC, PC, 128)
    total = None
    for dx in range(3):
        part = None
        for dy in range(3):
            moved = noise[dy : dy + EC - 2]
            if dy or dx:
                moved = pltpu.roll(moved, 8 * (3 * dy + dx), 2)
            part = moved if part is None else part + moved
        part = part[:, 3 + dx : 3 + dx + QC, :]
        total = part if total is None else total + part
    patch[...] = total.reshape((EC - 2) * QC, 128)

    def fill(even, odd, pitch, lane, first, last, window):
        for dx in range(3):
            for ref, start in ((even, first + first % 2), (odd, first + 1 - first % 2)):
                rows = last - first - 2 * (start != first)
                at = (start // 2) * 2 * pitch
                ref[dx, at : at + rows * pitch, lane : lane + 128] = window(start, rows, dx - 1).astype(BF16)

    def taps(even, odd, pitch, first, rows):
        parts = []
        for dy in range(3):
            start = first - 1 + dy
            ref = odd if start % 2 else even
            at = (start // 2) * 2 * pitch
            parts += [ref[dx, at : at + rows * pitch, :] for dx in range(3)]
        return parts

    def flat(ref, t, pitch):
        return lambda start, rows, shift: ref[t, pl.ds(PAD + start * pitch + shift, rows * pitch), :]

    def cells(ref, t, pitch, first, rows):
        return ref[t, pl.ds(PAD + first * pitch, rows * pitch), :]

    def valid(first, rows, pitch, row_own, col_own, scale):
        at = iota((rows, pitch, 128), 0) + (row_own * scale + first)
        col = iota((rows, pitch, 128), 1) + (col_own * scale)
        good = (at >= 0) & (at < GRID_ROWS * scale) & (col >= 0) & (col < GRID_COLS * scale)
        return good.reshape(rows * pitch, 128)

    def own_first(t, start, rows, shift):
        return jnp.concatenate(
            [first_h[t, pl.ds(PC * h + 4 + shift, QC), :] for h in range(start, start + rows)], 0
        )

    def coarse_left(first, rows):
        near = patch[QC * (first - 1) : QC * (first - 1 + rows), :].astype(BF16)
        return jnp.concatenate(taps(even_c, odd_c, QC, first, rows) + [near], 1)

    def coarse_gates(step):
        first, rows = 1 + 2 * step, 14 - 4 * step
        for t in range(3):
            if step == 0:
                window = functools.partial(own_first, t)
            else:
                window = flat(next_h, t, QC)
            fill(even_c, odd_c, QC, 128 * t, first - 1, first + rows + 1, window)
        operand = coarse_left(first, rows)
        gates = dot(operand, wg2[:, 0:512])
        for t in range(3):
            old = own_first(t, first, rows, 0) if step == 0 else cells(next_h, t, QC, first, rows)
            reset_h[t, pl.ds(PAD + QC * first, QC * rows), :] = sigmoid(gates[:, 128 * t : 128 * t + 128]) * old
        gate_u[0, pl.ds(PAD + QC * first, QC * rows), :] = sigmoid(gates[:, 384:512])
        gates = dot(coarse_left(first + 1, rows - 2), wg2[:, 512:768])
        for t in (1, 2):
            at = pl.ds(PAD + QC * (first + 1), QC * (rows - 2))
            gate_u[t, at, :] = sigmoid(gates[:, 128 * t - 128 : 128 * t])

    def coarse_cand(step):
        first, rows = 2 + 2 * step, 12 - 4 * step
        for t in range(3):
            fill(even_c, odd_c, QC, 128 * t, first - 1, first + rows + 1, flat(reset_h, t, QC))
        operand = coarse_left(first, rows)
        good = valid(first, rows, QC, row0 * RC - HC, col0 * CC - 4, 1)
        for lanes, here in ((slice(0, 256), (0, 1)), (slice(256, 384), (2,))):
            cand = jnp.tanh(dot(operand, wc2[:, lanes]))
            for i, t in enumerate(here):
                new = cand[:, 128 * i : 128 * i + 128]
                old = own_first(t, first, rows, 0) if step == 0 else cells(next_h, t, QC, first, rows)
                new = new + cells(gate_u, t, QC, first, rows) * (old - new)
                new = jnp.where(good, new, 0.0).astype(BF16).astype(F32)
                next_h[t, pl.ds(PAD + QC * first, QC * rows), :] = new

    def fine_input(step):
        first, rows = 3 + step, 10 - 2 * step
        state = jnp.concatenate(
            [
                jnp.concatenate(
                    [next_h[t, pl.ds(PAD + QC * h + 2, QC), :] for h in range(first, first + rows)], 0
                )
                for t in range(3)
            ],
            1,
        ).astype(BF16)
        value = dot(state, wup[...])
        for q in range(2):
            for p in range(2):
                lane = 256 * (2 * q + p)
                for r in range(rows):
                    at = PAD + (2 * (first + r) - 6 + q) * QF + p
                    tiles_put(fine_x, pl.ds(at, 20, stride=2), value[QC * r : QC * r + 20, lane : lane + 256])

    def fine_mixed(state, first, last):
        fill(even_f, odd_f, QF, 128, first, last, lambda *w: flat(fine_x, 1, QF)(*w) + flat(state, 0, QF)(*w))

    def fine_before(step):
        first, rows = 1 + 2 * step, 18 - 4 * step
        fill(even_f, odd_f, QF, 256, first - 1, first + rows + 1, flat(fine_h, 1, QF))

    def fine_gates(step):
        first, rows = 1 + 2 * step, 18 - 4 * step
        fill(even_f, odd_f, QF, 0, first - 1, first + rows + 1, flat(fine_x, 0, QF))
        fine_mixed(fine_h, first - 1, first + rows + 1)
        gates = dot(jnp.concatenate(taps(even_f, odd_f, QF, first, rows), 1), wr1[...])
        at = pl.ds(PAD + QF * first, QF * rows)
        gate = sigmoid(gates[:, 0:128])
        fine_reset[0, at, :] = gate * fine_h[0, at, :]
        fine_u[0, at, :] = pltpu.roll(gate, 64, 1)
        fine_reset[1, at, :] = sigmoid(gates[:, 128:256]) * fine_h[1, at, :]
        middle = jnp.concatenate(taps(even_f, odd_f, QF, first + 1, rows - 2)[1::3], 1)
        count = QF * (rows - 2)
        sides = dot(middle, wu1[...])
        for i in range(2):
            side_u[i, PAD : PAD + count, :] = sides[:, 128 * i : 128 * i + 128]
        gate = dot(middle, wv1[...]) + side_u[0, pl.ds(PAD - 1, count), :] + side_u[1, pl.ds(PAD + 1, count), :]
        fine_u[1, pl.ds(PAD + QF * (first + 1), count), :] = sigmoid(gate)

    def fine_cand():
        first, rows = 2, 16
        fine_mixed(fine_reset, first - 1, first + rows + 1)
        fill(even_f, odd_f, QF, 256, first - 1, first + rows + 1, flat(fine_reset, 1, QF))
        operand = jnp.concatenate(taps(even_f, odd_f, QF, first, rows), 1)
        good = valid(first, rows, QF, row0 * RC - HC + 3, col0 * CC - 2, 2)
        cand = jnp.tanh(dot_t(operand, wc1[...]))
        at = pl.ds(PAD + QF * first, QF * rows)
        for t in range(2):
            new = cand[:, 128 * t : 128 * t + 128]
            new = new + fine_u[t, at, :] * (fine_h[t, at, :] - new)
            fine_h[t, at, :] = jnp.where(good, new, 0.0).astype(BF16).astype(F32)

    def own_fine(ref, t, shift=0, first=HF, rows=RF):
        return jnp.concatenate(
            [ref[t, pl.ds(PAD + QF * h + HF + shift, CF), :] for h in range(first, first + rows)], 0
        )

    def fine_last():
        first, rows = HF - 1, RF + 2
        for dx in range(3):
            x1 = own_fine(fine_x, 1, dx - 1, first, rows) + own_fine(fine_reset, 0, dx - 1, first, rows)
            last_f[dx, :, 0:128] = own_fine(fine_x, 0, dx - 1, first, rows).astype(BF16)
            last_f[dx, :, 128:256] = x1.astype(BF16)
            last_f[dx, :, 256:384] = own_fine(fine_reset, 1, dx - 1, first, rows).astype(BF16)
        parts = [last_f[dx, CF * dy : CF * (dy + RF), :] for dy in range(3) for dx in range(3)]
        cand = jnp.tanh(dot_t(jnp.concatenate(parts, 1), wc1[...]))
        state = []
        for t in range(2):
            new = cand[:, 128 * t : 128 * t + 128]
            state.append(new + own_fine(fine_u, t) * (own_fine(fine_h, t) - new))
        return jnp.concatenate(state, 1).astype(BF16)

    def emit(step, state):
        rows = RF
        shape = (2 * rows, 8, 128)
        lane, cell = iota(shape, 2), iota(shape, 1)
        low, mine = lane < 64, ((lane >> 3) & 7) == cell
        lines = []
        for r in range(0, 8, 2):
            pair = dot_t(state, whead[128 * r : 128 * r + 256, :])
            for i in range(2):
                value = pair[:, 128 * i : 128 * i + 128].reshape(2 * rows, 2, 8, 128)
                lines.append(jnp.where(mine, jnp.where(low, value[:, 0], value[:, 1]), 0.0))
        for d in (1, 2, 4):
            here = (cell & d) == 0
            folded = []
            for i in range(0, len(lines), 2):
                a, b = lines[i], lines[i + 1]
                folded.append(jnp.where(here, a, b) + pltpu.roll(jnp.where(here, b, a), d, 1))
            lines = folded
        final = lines[0].reshape(rows, 2, 8, 128)
        for t in range(2):
            out[step, :, 128 * t : 128 * t + 128] = final[:, t].reshape(8 * rows, 128)

    coarse_gates(0)
    fine_before(0)
    coarse_cand(0)
    fine_input(0)
    coarse_gates(1)
    fine_gates(0)
    coarse_cand(1)
    fine_cand()
    fine_input(1)
    emit(0, jnp.concatenate([own_fine(fine_h, 0), own_fine(fine_h, 1)], 1).astype(BF16))
    fine_before(1)
    fine_gates(1)
    emit(1, fine_last())


def in_hbm(value):
    return pltpu.with_memory_space_constraint(value, pltpu.HBM)


def swapped(value, axis, odd):
    pairs = []
    for i in range(odd, lax.axis_size(axis) - 1, 2):
        pairs += [(i, i + 1), (i + 1, i)]
    return lax.ppermute(value, axis, pairs)


def call(kernel, out_shape, in_specs, scratch, limit, flops, bytes_accessed, **extra):
    return pl.pallas_call(
        kernel,
        out_shape=out_shape,
        in_specs=in_specs,
        out_specs=[VMEM] * len(out_shape),
        scratch_shapes=scratch,
        compiler_params=pltpu.CompilerParams(vmem_limit_bytes=limit),
        cost_estimate=pl.CostEstimate(flops=flops, bytes_accessed=bytes_accessed, transcendentals=0),
        **extra,
    )


def on_device(
    context_frames,
    latent_noise,
    latent_proj,
    coarse_context,
    fine_context,
    coarse_gates,
    coarse_candidate,
    fine_gates,
    fine_candidate,
    upsample_proj,
    head_proj,
):
    place = jnp.stack([lax.axis_index("row"), lax.axis_index("col")]).astype(jnp.int32)
    shape = jax.ShapeDtypeStruct
    row_buf, col_buf = shape((ROW_BUF, C2), BF16), shape((COL_BUF, C2), BF16)

    hc, hf, noise, even, odd = call(
        start_kernel,
        [
            shape((RC, CC, C2), BF16),
            shape((RF, CF, WF), BF16),
            shape((16, 128), BF16),
            row_buf,
            row_buf,
        ],
        [SMEM] + [HBM] * 4,
        [
            pltpu.VMEM((4, 16 * RC, 16 * CC), BF16),
            pltpu.VMEM((RC, 8, CC), BF16),
            pltpu.VMEM((1024, C2), BF16),
            pltpu.VMEM((WF, 256), BF16),
            pltpu.VMEM((2, 2, 128, 256), BF16),
            pltpu.VMEM((256, 256), BF16),
            pltpu.VMEM((2, 512, 256), BF16),
            pltpu.VMEM((ROW_BUF, C2), F32),
            pltpu.SemaphoreType.DMA((4,)),
        ],
        16 << 20, 10**9, 2 << 20,
    )(
        place,
        in_hbm(context_frames),
        in_hbm(latent_noise.transpose(0, 2, 1)),
        in_hbm(coarse_context),
        in_hbm(fine_context.T),
    )

    even, odd = swapped(even, "row", 0), swapped(odd, "row", 1)

    wg2, wc2, token = call(
        coarse_weights_kernel,
        [shape((KC, 2 * C2), BF16), shape((KC, C2), BF16), shape((8, 128), F32)],
        [HBM] * 3,
        [
            pltpu.VMEM((8, C2), BF16),
            pltpu.VMEM((TAPS, C2, 2 * C2), BF16),
            pltpu.VMEM((TAPS, C2, C2), BF16),
            pltpu.VMEM((128, 2 * C2), F32),
            pltpu.VMEM((128, C2), F32),
            pltpu.SemaphoreType.DMA((4 * TAPS + 1,)),
        ],
        16 << 20, 10**9, 24 << 20,
    )(in_hbm(latent_proj), in_hbm(coarse_gates), in_hbm(coarse_candidate))

    ec, ef, en, even, odd = call(
        column_kernel,
        [
            shape((EC, CC, C2), BF16),
            shape((EF, CF, WF), BF16),
            shape((EC, CC, 128), BF16),
            col_buf,
            col_buf,
        ],
        [SMEM] + [VMEM] * 5 + [ANY],
        [
            pltpu.VMEM((3, EC * CC, 128), F32),
            pltpu.VMEM((2, 24 * CF, 128), F32),
            pltpu.VMEM((EC * CC, 128), F32),
            pltpu.VMEM((COL_BUF, C2), F32),
        ],
        8 << 20, 10**6, 2 << 20,
    )(place, hc, hf, noise, even, odd, token)

    even, odd = swapped(even, "col", 0), swapped(odd, "col", 1)

    wr1, wu1, wv1, wc1, up, head = call(
        fine_weights_kernel,
        [
            shape((18 * C1, 256), BF16),
            shape((6 * C1, 256), BF16),
            shape((6 * C1, 128), BF16),
            shape((WF, 18 * C1), BF16),
            shape((C2, 1024), BF16),
            shape((1024, WF), BF16),
        ],
        [ANY] + [HBM] * 4,
        [
            pltpu.VMEM((18 * C1, 2 * C1), BF16),
            pltpu.VMEM((C2, 4 * C1), BF16),
            pltpu.VMEM((64, C1), BF16),
            pltpu.SemaphoreType.DMA((4,)),
        ],
        12 << 20, 10**8, 8 << 20,
    )(en, in_hbm(fine_gates), in_hbm(fine_candidate.T), in_hbm(upsample_proj), in_hbm(head_proj.T))

    (forecast,) = call(
        main_kernel,
        [shape((2, 96, 256), F32)],
        [SMEM] + [VMEM] * 13,
        [
            pltpu.VMEM((3, EC * PC, 128), F32),
            pltpu.VMEM((EC * PC, 128), F32),
            pltpu.VMEM(((EC - 2) * QC, 128), F32),
            pltpu.VMEM((3, PAD + EC * QC + 8, 128), F32),
            pltpu.VMEM((3, PAD + EC * QC + 8, 128), F32),
            pltpu.VMEM((3, PAD + EC * QC + 8, 128), F32),
            pltpu.VMEM((2, PAD + EF * QF + 8, 128), F32),
            pltpu.VMEM((2, PAD + EF * QF + 8, 128), F32),
            pltpu.VMEM((2, PAD + EF * QF + 8, 128), F32),
            pltpu.VMEM((2, PAD + EF * QF + 8, 128), F32),
            pltpu.VMEM((2, PAD + 16 * QF + 8, 128), F32),
            pltpu.VMEM((3, EC * QC, C2), BF16),
            pltpu.VMEM((3, EC * QC, C2), BF16),
            pltpu.VMEM((3, EF * QF, 2 * C1), BF16),
            pltpu.VMEM((3, EF * QF, 2 * C1), BF16),
            pltpu.VMEM((3, (RF + 2) * CF, 2 * C1), BF16),
        ],
        26 << 20, 9 * 10**9, 30 << 20,
    )(place, ec, ef, en, even, odd, wg2, wc2, wr1, wu1, wv1, wc1, up, head)
    return forecast


def solution(mesh):
    return jax.shard_map(
        on_device,
        mesh=mesh,
        in_specs=(
            P(None, "row", "col"),
            P("row", "col", None),
            P(),
            P(),
            P(),
            P(),
            P(),
            P(),
            P(),
            P(),
            P(),
        ),
        out_specs=P(None, "row", "col"),
        check_vma=False,
    )
```

```python
import functools

import jax
import jax.numpy as jnp
from jax import lax
from jax.experimental import pallas as pl
from jax.experimental.pallas import tpu as pltpu
from jax.sharding import PartitionSpec as P

F32 = jnp.float32
BF16 = jnp.bfloat16

C2, C1 = 384, 192
GRID_ROWS, GRID_COLS = 48, 256
RC, CC = 6, 16
RF, CF = 12, 32
HC, HF = 5, 4
EC, EF = RC + 2 * HC, RF + 2 * HF
PC = 32
QC, QF = 24, 40
PAD = 8
WF = 256
ROW_BUF, COL_BUF = 160, 144
TAPS = 9
KC = TAPS * C2 + 128

VMEM = pl.BlockSpec(memory_space=pltpu.VMEM)
SMEM = pl.BlockSpec(memory_space=pltpu.SMEM)
ANY = pl.BlockSpec(memory_space=pl.ANY)
HBM = pl.BlockSpec(memory_space=pltpu.HBM)


def dot(a, b):
    return jnp.dot(a, b, preferred_element_type=F32)


def dot_t(a, b):
    return lax.dot_general(a, b, (((1,), (1,)), ((), ())), preferred_element_type=F32)


def sigmoid(x):
    return 0.5 * jnp.tanh(0.5 * x) + 0.5


def iota(shape, dim):
    return lax.broadcasted_iota(jnp.int32, shape, dim)


def tiles_get(ref, rows):
    return jnp.concatenate([ref[t, rows, :] for t in range(ref.shape[0])], 1)


def pack_pair(a, b):
    return jnp.concatenate([a[:, 128:], b[:, 128:], a[:, :128] + pltpu.roll(b[:, :128], 64, 1)], 1)


def unpack_pair(both):
    mixed = both[:, 256:384]
    upper = iota(mixed.shape, 1) >= 64
    a = jnp.where(upper, mixed, 0.0)
    b = jnp.where(upper, pltpu.roll(mixed, 64, 1), 0.0)
    return jnp.concatenate([a, both[:, :128]], 1), jnp.concatenate([b, both[:, 128:256]], 1)


def tiles_put(ref, rows, value):
    lanes = ref.shape[0] * 128
    if value.shape[1] < lanes:
        value = jnp.concatenate([value, jnp.zeros((value.shape[0], lanes - value.shape[1]), F32)], 1)
    for t in range(ref.shape[0]):
        ref[t, rows, :] = value[:, 128 * t : 128 * t + 128]


def indicator(cond):
    return jnp.where(cond, 1.0, 0.0).astype(BF16)


def start_kernel(
    place,
    frames_hbm,
    noise_hbm,
    context2_hbm,
    context1_hbm,
    cand_hbm,
    gates_hbm,
    hc_out,
    hf_out,
    noise_out,
    even_out,
    odd_out,
    cand_out,
    gates_out,
    frames,
    noise,
    context2,
    context1,
    picks,
    swaps,
    spreads,
    buf,
    sem,
):
    moves = [
        pltpu.make_async_copy(src, dst, sem.at[i])
        for i, (src, dst) in enumerate(
            (
                (frames_hbm, frames),
                (context2_hbm, context2),
                (context1_hbm, context1.at[pl.ds(WF - C1, C1), :]),
                (noise_hbm, noise),
            )
        )
    ]
    weights = [
        pltpu.make_async_copy(
            cand_hbm.at[pl.ds(2 * C2 * t + C2, C2), :], cand_out.at[pl.ds(C2 * t, C2), :], sem.at[4 + t]
        )
        for t in range(TAPS)
    ]
    weights.append(pltpu.make_async_copy(gates_hbm, gates_out, sem.at[4 + TAPS]))
    for copy in moves + weights:
        copy.start()

    def pick(shift, parity):
        row, col = iota((128, 256), 0), iota((128, 256), 1)
        count = 256 >> shift
        j = 2 * (row >> (8 - shift)) + parity
        return indicator(col == ((row & (count - 1)) << shift) + j)

    context1[0 : WF - C1, :] = jnp.zeros((WF - C1, 256), BF16)
    for shift in (4, 3):
        for parity in range(2):
            picks[4 - shift, parity] = pick(shift, parity)
    row, col = iota((256, 256), 0), iota((256, 256), 1)
    swaps[...] = indicator(col == ((row & 15) << 4) + (row >> 4))
    row, col = iota((512, 256), 0), iota((512, 256), 1)
    source = (((row >> 4) & 3) << 6) + ((row & 7) << 3) + (row >> 6)
    for q in range(2):
        spreads[q] = indicator((col == source) & (((row >> 3) & 1) == q))
    moves[0].wait()
    zeros = jnp.zeros((64, 256), BF16)
    even, odd = [], []
    for r in range(RC):
        band = frames[:, 16 * r : 16 * r + 16, :].reshape(64, 256)
        even += [band, zeros]
        odd += [zeros, band]
    even, odd = jnp.concatenate(even, 0), jnp.concatenate(odd, 0)

    def turned(shift):
        both = dot_t(picks[4 - shift, 0], even) + dot_t(picks[4 - shift, 1], odd)
        return both.astype(BF16)

    deep = turned(3)
    left = jnp.concatenate(
        [
            jnp.concatenate([deep[32 * j : 32 * j + 32, 128 * r : 128 * r + 128] for r in range(RC)], 0)
            for j in range(4)
        ],
        1,
    )
    moves[2].wait()
    for q in range(2):
        weight = dot_t(spreads[q], context1[...]).astype(BF16)
        state1 = jnp.tanh(dot(left, weight)).astype(BF16)
        for r in range(RC):
            hf_out[2 * r + q] = state1[CF * r : CF * r + CF]

    deep = turned(4)
    left = jnp.concatenate(
        [
            jnp.concatenate([deep[16 * j : 16 * j + 16, 128 * r : 128 * r + 128] for r in range(RC)], 0)
            for j in range(8)
        ],
        1,
    )
    moves[1].wait()
    swap = swaps[...]
    moved = [dot(swap, context2[256 * f : 256 * f + 256, :]).astype(BF16) for f in range(4)]
    weight = jnp.concatenate([moved[f][16 * j : 16 * j + 16] for j in range(16) for f in range(4)], 0)
    state2 = jnp.tanh(dot(left, weight))
    hc_out[...] = state2.astype(BF16).reshape(RC, CC, C2)

    moves[3].wait()
    diagonal = indicator(iota((16, 16), 0) == iota((16, 16), 1))
    turned_noise = dot_t(diagonal, noise[...].reshape(RC * 8, CC))
    turned_noise = jnp.concatenate([turned_noise, jnp.zeros((16, 128 - 8 * RC), F32)], 1)
    noise_out[...] = turned_noise.astype(BF16)
    low_noise = pltpu.roll(turned_noise, 128 - 8 * (RC - HC), 1)

    up_first = (place[0] & 1) == 1
    for target, up in ((even_out, up_first), (odd_out, jnp.logical_not(up_first))):
        c_top = state2[: HC * CC]
        c_low = state2[(RC - HC) * CC :]
        buf[0:80, :] = jnp.where(up, c_top, c_low)
        top = [hf_out[r : r + 2].reshape(64, WF).astype(F32) for r in (0, 2)]
        low = [hf_out[r : r + 2].reshape(64, WF).astype(F32) for r in (RF - HF, RF - HF + 2)]
        buf[80:144, :] = jnp.where(up, pack_pair(*top), pack_pair(*low))
        buf[144:160, :] = jnp.zeros((16, C2), F32)
        buf[144:160, 0:128] = jnp.where(up, turned_noise, low_noise)
        target[...] = buf[...].astype(BF16)
    for copy in weights:
        copy.wait()


def column_kernel(
    place, hc, hf, noise, odd_in, even_in, after, ec_out, ef_out, en_out, even_out, odd_out, sc, sf, sn, buf
):
    up_first = (place[0] & 1) == 1
    above = jnp.where(up_first, even_in[...].astype(F32), odd_in[...].astype(F32))
    below = jnp.where(up_first, odd_in[...].astype(F32), even_in[...].astype(F32))
    tiles_put(sc, pl.ds(0, 80), above[0:80])
    tiles_put(sc, pl.ds(80, 96), hc[...].reshape(RC * CC, C2).astype(F32))
    tiles_put(sc, pl.ds(176, 80), below[0:80])
    for half, strip in enumerate(unpack_pair(above[80:144])):
        tiles_put(sf, pl.ds(64 * half, 64), strip)
    for half, strip in enumerate(unpack_pair(below[80:144])):
        tiles_put(sf, pl.ds(512 + 64 * half, 64), strip)
    tiles_put(sf, pl.ds(128, 384), hf[...].reshape(RF * CF, WF).astype(F32))
    tiles_put(sf, pl.ds(640, 128), jnp.zeros((128, WF), F32))
    sn[...] = jnp.zeros(sn.shape, F32)
    for h in range(HC):
        sn[16 * h : 16 * h + 16, 0:8] = above[144:160, 8 * h : 8 * h + 8]
        sn[16 * (HC + RC + h) : 16 * (HC + RC + h) + 16, 0:8] = below[144:160, 8 * h : 8 * h + 8]
    for h in range(RC):
        sn[16 * (HC + h) : 16 * (HC + h) + 16, 0:8] = noise[:, 8 * h : 8 * h + 8].astype(F32)

    ec_out[...] = tiles_get(sc, pl.ds(0, EC * CC)).astype(BF16).reshape(EC, CC, C2)
    ef_out[...] = tiles_get(sf, pl.ds(0, EF * CF)).astype(BF16).reshape(EF, CF, WF)
    en_out[...] = sn[...].astype(BF16).reshape(EC, CC, 128)

    left_first = (place[1] & 1) == 1
    for target, left in ((even_out, left_first), (odd_out, jnp.logical_not(left_first))):
        c_from = jnp.where(left, 0, CC - HC)
        f_from = jnp.where(left, 0, CF - HF)
        buf[128:144, :] = jnp.zeros((16, C2), F32)
        for k in range(HC):
            buf[16 * k : 16 * k + 16, :] = tiles_get(sc, pl.ds(c_from + k, 16, stride=CC))
            strip = sn[pl.ds(c_from + k, 16, stride=CC), :]
            buf[128:144, 8 * k : 8 * k + 8] = strip[:, 0:8]
        for k in range(2):
            strips = [tiles_get(sf, pl.ds(f_from + i, 24, stride=CF)) for i in (k, k + 2)]
            buf[80 + 24 * k : 104 + 24 * k, :] = pack_pair(*strips)
        target[...] = buf[...].astype(BF16)


def coarse_weights_kernel(
    proj_hbm, gates_hbm, cand_hbm, wg_out, wc_out, token, proj, gates, cand, acc_g, acc_c, sem
):
    count = [0]

    def move(src, dst):
        copy = pltpu.make_async_copy(src, dst, sem.at[count[0]])
        count[0] += 1
        copy.start()
        return copy

    first = move(proj_hbm, proj)
    inputs, states = [], []
    for hbm, held in ((gates_hbm, gates), (cand_hbm, cand)):
        inputs.append([move(hbm.at[pl.ds(2 * C2 * t, C2), :], held.at[t]) for t in range(TAPS)])
    for t in range(TAPS):
        states.append(move(gates_hbm.at[pl.ds(2 * C2 * t + C2, C2), :], wg_out.at[pl.ds(C2 * t, C2), :]))
    acc_g[...] = jnp.zeros(acc_g.shape, F32)
    acc_c[...] = jnp.zeros(acc_c.shape, F32)
    first.wait()
    token[...] = jnp.zeros(token.shape, F32)
    wide = jnp.concatenate([proj[...].astype(F32), jnp.zeros((8, C2), F32)], 0).astype(BF16)
    for copies, held, acc in ((inputs[0], gates, acc_g), (inputs[1], cand, acc_c)):
        for t in range(TAPS):
            copies[t].wait()
            acc[8 * t : 8 * t + 8, :] = dot(wide, held[t])[0:8]
    wg_out[TAPS * C2 :, :] = acc_g[...].astype(BF16)
    wc_out[...] = acc_c[...].astype(BF16)
    for copy in states:
        copy.wait()


def fine_weights_kernel(
    after, gates, cand_hbm, up_hbm, head_hbm, wr_out, wu_out, wv_out, wc_out, up_out, head_out, up, head, sem
):
    moves = [
        pltpu.make_async_copy(src, dst, sem.at[i])
        for i, (src, dst) in enumerate(
            (
                (up_hbm, up),
                (head_hbm, head),
                (cand_hbm, wc_out.at[pl.ds(WF - C1, C1), :]),
            )
        )
    ]
    for copy in moves:
        copy.start()
    wc_out[0 : WF - C1, :] = jnp.zeros((WF - C1, 18 * C1), BF16)
    moves[1].wait()
    row, col = iota((1024, 64), 0), iota((1024, 64), 1)
    spread = indicator(col == ((row >> 7) << 3) + (row & 7))
    wide = jnp.concatenate([jnp.zeros((64, WF - C1), F32), head[...].astype(F32)], 1).astype(BF16)
    head_out[...] = dot(spread, wide).astype(BF16)
    moves[0].wait()
    wide = up[...].astype(F32)
    zeros = jnp.zeros((C2, 256 - C1), F32)
    for i in range(4):
        part = jnp.concatenate([wide[:, C1 * i : C1 * i + C1], zeros], 1)
        up_out[:, 256 * i : 256 * i + 256] = part.astype(BF16)
    for t in range(TAPS):
        rows = slice(2 * C1 * t, 2 * C1 * t + 2 * C1)
        part = gates[rows, 0:256].astype(F32)
        wr_out[rows, :] = jnp.concatenate([part[:, C1:256], part[:, :C1]], 1).astype(BF16)
        target, lane = (wv_out, 0) if t % 3 == 1 else (wu_out, 64 * (t % 3))
        target[2 * C1 * (t // 3) : 2 * C1 * (t // 3) + 2 * C1, lane : lane + 128] = gates[rows, 256:384]
    moves[2].wait()


def main_kernel(
    place,
    ec,
    ef,
    en,
    odd_in,
    even_in,
    wg2,
    wc2,
    fold2,
    wr1,
    wu1,
    wv1,
    wc1,
    wup,
    whead,
    out,
    first_h,
    sn,
    patch,
    reset_h,
    next_h,
    gate_u,
    fine_x,
    fine_h,
    fine_reset,
    fine_u,
    side_u,
    even_c,
    odd_c,
    even_f,
    odd_f,
    last_f,
):
    row0, col0 = place[0], place[1]
    left_first = (col0 & 1) == 1
    left = jnp.where(left_first, even_in[...].astype(F32), odd_in[...].astype(F32))
    right = jnp.where(left_first, odd_in[...].astype(F32), even_in[...].astype(F32))

    for ref, pitch, rows in (
        (reset_h, QC, EC), (next_h, QC, EC), (fine_x, QF, EF), (fine_h, QF, EF), (fine_reset, QF, EF)
    ):
        for t in range(ref.shape[0]):
            ref[t, 0 : PAD + 2 * pitch, :] = jnp.zeros((PAD + 2 * pitch, 128), F32)
            ref[t, PAD + (rows - 2) * pitch :, :] = jnp.zeros((2 * pitch + 8, 128), F32)
    sn[...] = jnp.zeros(sn.shape, F32)
    for h in range(EC):
        tiles_put(first_h, pl.ds(PC * h + 8, CC), ec[h].astype(F32))
        sn[PC * h + 8 : PC * h + 24, :] = en[h].astype(F32)
    for k in range(HC):
        for side, at in ((left, 8 - HC + k), (right, 8 + CC + k)):
            tiles_put(first_h, pl.ds(at, EC, stride=PC), side[16 * k : 16 * k + 16])
            strip = jnp.concatenate([side[128:144, 8 * k : 8 * k + 8], jnp.zeros((16, 120), F32)], 1)
            sn[pl.ds(at, EC, stride=PC), :] = strip
    for h in range(EF):
        tiles_put(fine_h, pl.ds(PAD + QF * h + HF, CF), ef[h].astype(F32))
    for side, col in ((left, 0), (right, HF + CF)):
        for k in range(2):
            for i, strip in enumerate(unpack_pair(side[80 + 24 * k : 80 + 24 * k + EF])):
                tiles_put(fine_h, pl.ds(PAD + col + k + 2 * i, EF, stride=QF), strip)

    noise = sn[...].reshape(EC, PC, 128)
    total = None
    for dx in range(3):
        part = None
        for dy in range(3):
            moved = noise[dy : dy + EC - 2]
            if dy or dx:
                moved = pltpu.roll(moved, 8 * (3 * dy + dx), 2)
            part = moved if part is None else part + moved
        part = part[:, 3 + dx : 3 + dx + QC, :]
        total = part if total is None else total + part
    patch[...] = total.reshape((EC - 2) * QC, 128)

    def fill(even, odd, pitch, lane, first, last, window):
        for dx in range(3):
            for ref, start in ((even, first + first % 2), (odd, first + 1 - first % 2)):
                rows = last - first - 2 * (start != first)
                at = (start // 2) * 2 * pitch
                ref[dx, at : at + rows * pitch, lane : lane + 128] = window(start, rows, dx - 1).astype(BF16)

    def taps(even, odd, pitch, first, rows):
        parts = []
        for dy in range(3):
            start = first - 1 + dy
            ref = odd if start % 2 else even
            at = (start // 2) * 2 * pitch
            parts += [ref[dx, at : at + rows * pitch, :] for dx in range(3)]
        return parts

    def flat(ref, t, pitch):
        return lambda start, rows, shift: ref[t, pl.ds(PAD + start * pitch + shift, rows * pitch), :]

    def cells(ref, t, pitch, first, rows):
        return ref[t, pl.ds(PAD + first * pitch, rows * pitch), :]

    def valid(first, rows, pitch, row_own, col_own, scale):
        at = iota((rows, pitch, 128), 0) + (row_own * scale + first)
        col = iota((rows, pitch, 128), 1) + (col_own * scale)
        good = (at >= 0) & (at < GRID_ROWS * scale) & (col >= 0) & (col < GRID_COLS * scale)
        return good.reshape(rows * pitch, 128)

    def own_first(t, start, rows, shift):
        return jnp.concatenate(
            [first_h[t, pl.ds(PC * h + 4 + shift, QC), :] for h in range(start, start + rows)], 0
        )

    def coarse_left(first, rows):
        near = patch[QC * (first - 1) : QC * (first - 1 + rows), :].astype(BF16)
        return jnp.concatenate(taps(even_c, odd_c, QC, first, rows) + [near], 1)

    def coarse_ready(step):
        first, rows = 1 + 2 * step, 14 - 4 * step
        for t in range(3):
            if step == 0:
                window = functools.partial(own_first, t)
            else:
                window = flat(next_h, t, QC)
            fill(even_c, odd_c, QC, 128 * t, first - 1, first + rows + 1, window)

    def coarse_gates(step):
        first, rows = 1 + 2 * step, 14 - 4 * step
        operand = coarse_left(first, rows)
        gates = dot(operand, wg2[:, 0:512])
        for t in range(3):
            old = own_first(t, first, rows, 0) if step == 0 else cells(next_h, t, QC, first, rows)
            reset_h[t, pl.ds(PAD + QC * first, QC * rows), :] = sigmoid(gates[:, 128 * t : 128 * t + 128]) * old
        gate_u[0, pl.ds(PAD + QC * first, QC * rows), :] = sigmoid(gates[:, 384:512])
        gates = dot(coarse_left(first + 1, rows - 2), wg2[:, 512:768])
        for t in (1, 2):
            at = pl.ds(PAD + QC * (first + 1), QC * (rows - 2))
            gate_u[t, at, :] = sigmoid(gates[:, 128 * t - 128 : 128 * t])

    def coarse_cand(step):
        first, rows = 2 + 2 * step, 12 - 4 * step
        for t in range(3):
            fill(even_c, odd_c, QC, 128 * t, first - 1, first + rows + 1, flat(reset_h, t, QC))
        operand = coarse_left(first, rows)
        good = valid(first, rows, QC, row0 * RC - HC, col0 * CC - 4, 1)
        for lanes, here in ((slice(0, 256), (0, 1)), (slice(256, 384), (2,))):
            cand = jnp.tanh(dot(operand, jnp.concatenate([wc2[:, lanes], fold2[:, lanes]], 0)))
            for i, t in enumerate(here):
                new = cand[:, 128 * i : 128 * i + 128]
                old = own_first(t, first, rows, 0) if step == 0 else cells(next_h, t, QC, first, rows)
                new = new + cells(gate_u, t, QC, first, rows) * (old - new)
                new = jnp.where(good, new, 0.0).astype(BF16).astype(F32)
                next_h[t, pl.ds(PAD + QC * first, QC * rows), :] = new

    def fine_input(step):
        first, rows = 3 + step, 10 - 2 * step
        state = jnp.concatenate(
            [
                jnp.concatenate(
                    [next_h[t, pl.ds(PAD + QC * h + 2, QC), :] for h in range(first, first + rows)], 0
                )
                for t in range(3)
            ],
            1,
        ).astype(BF16)
        value = dot(state, wup[...])
        for q in range(2):
            for p in range(2):
                lane = 256 * (2 * q + p)
                for r in range(rows):
                    at = PAD + (2 * (first + r) - 6 + q) * QF + p
                    tiles_put(fine_x, pl.ds(at, 20, stride=2), value[QC * r : QC * r + 20, lane : lane + 256])

    def fine_mixed(state, first, last):
        fill(even_f, odd_f, QF, 128, first, last, lambda *w: flat(fine_x, 1, QF)(*w) + flat(state, 0, QF)(*w))

    def fine_before(step):
        first, rows = 1 + 2 * step, 18 - 4 * step
        fill(even_f, odd_f, QF, 256, first - 1, first + rows + 1, flat(fine_h, 1, QF))

    def fine_ready(step):
        first, rows = 1 + 2 * step, 18 - 4 * step
        fill(even_f, odd_f, QF, 0, first - 1, first + rows + 1, flat(fine_x, 0, QF))
        fine_mixed(fine_h, first - 1, first + rows + 1)

    def fine_gates(step):
        first, rows = 1 + 2 * step, 18 - 4 * step
        gates = dot(jnp.concatenate(taps(even_f, odd_f, QF, first, rows), 1), wr1[...])
        at = pl.ds(PAD + QF * first, QF * rows)
        gate = sigmoid(gates[:, 0:128])
        fine_reset[0, at, :] = gate * fine_h[0, at, :]
        fine_u[0, at, :] = pltpu.roll(gate, 64, 1)
        fine_reset[1, at, :] = sigmoid(gates[:, 128:256]) * fine_h[1, at, :]
        middle = jnp.concatenate(taps(even_f, odd_f, QF, first + 1, rows - 2)[1::3], 1)
        count = QF * (rows - 2)
        sides = dot(middle, wu1[...])
        for i in range(2):
            side_u[i, PAD : PAD + count, :] = sides[:, 128 * i : 128 * i + 128]
        gate = dot(middle, wv1[...]) + side_u[0, pl.ds(PAD - 1, count), :] + side_u[1, pl.ds(PAD + 1, count), :]
        fine_u[1, pl.ds(PAD + QF * (first + 1), count), :] = sigmoid(gate)

    def fine_cand_ready():
        first, rows = 2, 16
        fine_mixed(fine_reset, first - 1, first + rows + 1)
        fill(even_f, odd_f, QF, 256, first - 1, first + rows + 1, flat(fine_reset, 1, QF))

    def fine_cand():
        first, rows = 2, 16
        operand = jnp.concatenate(taps(even_f, odd_f, QF, first, rows), 1)
        good = valid(first, rows, QF, row0 * RC - HC + 3, col0 * CC - 2, 2)
        cand = jnp.tanh(dot_t(operand, wc1[...]))
        at = pl.ds(PAD + QF * first, QF * rows)
        for t in range(2):
            new = cand[:, 128 * t : 128 * t + 128]
            new = new + fine_u[t, at, :] * (fine_h[t, at, :] - new)
            fine_h[t, at, :] = jnp.where(good, new, 0.0).astype(BF16).astype(F32)

    def own_fine(ref, t, shift=0, first=HF, rows=RF):
        return jnp.concatenate(
            [ref[t, pl.ds(PAD + QF * h + HF + shift, CF), :] for h in range(first, first + rows)], 0
        )

    def fine_last():
        first, rows = HF - 1, RF + 2
        for dx in range(3):
            x1 = own_fine(fine_x, 1, dx - 1, first, rows) + own_fine(fine_reset, 0, dx - 1, first, rows)
            last_f[dx, :, 0:128] = own_fine(fine_x, 0, dx - 1, first, rows).astype(BF16)
            last_f[dx, :, 128:256] = x1.astype(BF16)
            last_f[dx, :, 256:384] = own_fine(fine_reset, 1, dx - 1, first, rows).astype(BF16)
        parts = [last_f[dx, CF * dy : CF * (dy + RF), :] for dy in range(3) for dx in range(3)]
        cand = jnp.tanh(dot_t(jnp.concatenate(parts, 1), wc1[...]))
        state = []
        for t in range(2):
            new = cand[:, 128 * t : 128 * t + 128]
            state.append(new + own_fine(fine_u, t) * (own_fine(fine_h, t) - new))
        return jnp.concatenate(state, 1).astype(BF16)

    def emit(step, state):
        rows = RF
        shape = (2 * rows, 8, 128)
        lane, cell = iota(shape, 2), iota(shape, 1)
        low, mine = lane < 64, ((lane >> 3) & 7) == cell
        lines = []
        for r in range(0, 8, 2):
            pair = dot_t(state, whead[128 * r : 128 * r + 256, :])
            for i in range(2):
                value = pair[:, 128 * i : 128 * i + 128].reshape(2 * rows, 2, 8, 128)
                lines.append(jnp.where(mine, jnp.where(low, value[:, 0], value[:, 1]), 0.0))
        for d in (1, 2, 4):
            here = (cell & d) == 0
            folded = []
            for i in range(0, len(lines), 2):
                a, b = lines[i], lines[i + 1]
                folded.append(jnp.where(here, a, b) + pltpu.roll(jnp.where(here, b, a), d, 1))
            lines = folded
        final = lines[0].reshape(rows, 2, 8, 128)
        for t in range(2):
            out[step, :, 128 * t : 128 * t + 128] = final[:, t].reshape(8 * rows, 128)

    coarse_ready(0)
    coarse_gates(0)
    fine_before(0)
    coarse_cand(0)
    fine_input(0)
    coarse_ready(1)
    coarse_gates(1)
    fine_ready(0)
    fine_gates(0)
    coarse_cand(1)
    fine_cand_ready()
    fine_cand()
    fine_input(1)
    fine_before(1)
    fine_ready(1)
    fine_gates(1)
    emit(0, jnp.concatenate([own_fine(fine_h, 0), own_fine(fine_h, 1)], 1).astype(BF16))
    emit(1, fine_last())


def in_hbm(value):
    return pltpu.with_memory_space_constraint(value, pltpu.HBM)


def swapped(value, axis, odd):
    pairs = []
    for i in range(odd, lax.axis_size(axis) - 1, 2):
        pairs += [(i, i + 1), (i + 1, i)]
    return lax.ppermute(value, axis, pairs)


def call(kernel, out_shape, in_specs, scratch, limit, flops, bytes_accessed, **extra):
    return pl.pallas_call(
        kernel,
        out_shape=out_shape,
        in_specs=in_specs,
        out_specs=[VMEM] * len(out_shape),
        scratch_shapes=scratch,
        compiler_params=pltpu.CompilerParams(vmem_limit_bytes=limit),
        cost_estimate=pl.CostEstimate(flops=flops, bytes_accessed=bytes_accessed, transcendentals=0),
        **extra,
    )


def on_device(
    context_frames,
    latent_noise,
    latent_proj,
    coarse_context,
    fine_context,
    coarse_gates,
    coarse_candidate,
    fine_gates,
    fine_candidate,
    upsample_proj,
    head_proj,
):
    place = jnp.stack([lax.axis_index("row"), lax.axis_index("col")]).astype(jnp.int32)
    shape = jax.ShapeDtypeStruct
    row_buf, col_buf = shape((ROW_BUF, C2), BF16), shape((COL_BUF, C2), BF16)

    hc, hf, noise, even, odd, wc2, gates1 = call(
        start_kernel,
        [
            shape((RC, CC, C2), BF16),
            shape((RF, CF, WF), BF16),
            shape((16, 128), BF16),
            row_buf,
            row_buf,
            shape((TAPS * C2, C2), BF16),
            shape((18 * C1, 2 * C1), BF16),
        ],
        [SMEM] + [HBM] * 6,
        [
            pltpu.VMEM((4, 16 * RC, 16 * CC), BF16),
            pltpu.VMEM((RC, 8, CC), BF16),
            pltpu.VMEM((1024, C2), BF16),
            pltpu.VMEM((WF, 256), BF16),
            pltpu.VMEM((2, 2, 128, 256), BF16),
            pltpu.VMEM((256, 256), BF16),
            pltpu.VMEM((2, 512, 256), BF16),
            pltpu.VMEM((ROW_BUF, C2), F32),
            pltpu.SemaphoreType.DMA((5 + TAPS,)),
        ],
        16 << 20, 10**9, 8 << 20,
    )(
        place,
        in_hbm(context_frames),
        in_hbm(latent_noise.transpose(0, 2, 1)),
        in_hbm(coarse_context),
        in_hbm(fine_context.T),
        in_hbm(coarse_candidate),
        in_hbm(fine_gates),
    )

    odd = swapped(odd, "row", 1)
    even = swapped(even, "row", 0)

    wg2, fold2, token = call(
        coarse_weights_kernel,
        [shape((KC, 2 * C2), BF16), shape((128, C2), BF16), shape((8, 128), F32)],
        [HBM] * 3,
        [
            pltpu.VMEM((8, C2), BF16),
            pltpu.VMEM((TAPS, C2, 2 * C2), BF16),
            pltpu.VMEM((TAPS, C2, C2), BF16),
            pltpu.VMEM((128, 2 * C2), F32),
            pltpu.VMEM((128, C2), F32),
            pltpu.SemaphoreType.DMA((3 * TAPS + 1,)),
        ],
        16 << 20, 10**9, 24 << 20,
    )(in_hbm(latent_proj), in_hbm(coarse_gates), in_hbm(coarse_candidate))

    ec, ef, en, even, odd = call(
        column_kernel,
        [
            shape((EC, CC, C2), BF16),
            shape((EF, CF, WF), BF16),
            shape((EC, CC, 128), BF16),
            col_buf,
            col_buf,
        ],
        [SMEM] + [VMEM] * 5 + [ANY],
        [
            pltpu.VMEM((3, EC * CC, 128), F32),
            pltpu.VMEM((2, 24 * CF, 128), F32),
            pltpu.VMEM((EC * CC, 128), F32),
            pltpu.VMEM((COL_BUF, C2), F32),
        ],
        8 << 20, 10**6, 2 << 20,
    )(place, hc, hf, noise, odd, even, token)

    odd = swapped(odd, "col", 1)
    even = swapped(even, "col", 0)

    wr1, wu1, wv1, wc1, up, head = call(
        fine_weights_kernel,
        [
            shape((18 * C1, 256), BF16),
            shape((6 * C1, 256), BF16),
            shape((6 * C1, 128), BF16),
            shape((WF, 18 * C1), BF16),
            shape((C2, 1024), BF16),
            shape((1024, WF), BF16),
        ],
        [ANY, VMEM] + [HBM] * 3,
        [
            pltpu.VMEM((C2, 4 * C1), BF16),
            pltpu.VMEM((64, C1), BF16),
            pltpu.SemaphoreType.DMA((4,)),
        ],
        12 << 20, 10**8, 8 << 20,
    )(en, gates1, in_hbm(fine_candidate.T), in_hbm(upsample_proj), in_hbm(head_proj.T))

    (forecast,) = call(
        main_kernel,
        [shape((2, 96, 256), F32)],
        [SMEM] + [VMEM] * 14,
        [
            pltpu.VMEM((3, EC * PC, 128), F32),
            pltpu.VMEM((EC * PC, 128), F32),
            pltpu.VMEM(((EC - 2) * QC, 128), F32),
            pltpu.VMEM((3, PAD + EC * QC + 8, 128), F32),
            pltpu.VMEM((3, PAD + EC * QC + 8, 128), F32),
            pltpu.VMEM((3, PAD + EC * QC + 8, 128), F32),
            pltpu.VMEM((2, PAD + EF * QF + 8, 128), F32),
            pltpu.VMEM((2, PAD + EF * QF + 8, 128), F32),
            pltpu.VMEM((2, PAD + EF * QF + 8, 128), F32),
            pltpu.VMEM((2, PAD + EF * QF + 8, 128), F32),
            pltpu.VMEM((2, PAD + 16 * QF + 8, 128), F32),
            pltpu.VMEM((3, EC * QC, C2), BF16),
            pltpu.VMEM((3, EC * QC, C2), BF16),
            pltpu.VMEM((3, EF * QF, 2 * C1), BF16),
            pltpu.VMEM((3, EF * QF, 2 * C1), BF16),
            pltpu.VMEM((3, (RF + 2) * CF, 2 * C1), BF16),
        ],
        26 << 20, 9 * 10**9, 30 << 20,
    )(place, ec, ef, en, odd, even, wg2, wc2, fold2, wr1, wu1, wv1, wc1, up, head)
    return forecast


def solution(mesh):
    return jax.shard_map(
        on_device,
        mesh=mesh,
        in_specs=(
            P(None, "row", "col"),
            P("row", "col", None),
            P(),
            P(),
            P(),
            P(),
            P(),
            P(),
            P(),
            P(),
            P(),
        ),
        out_specs=P(None, "row", "col"),
        check_vma=False,
    )
```

```python
import functools

import jax
import jax.numpy as jnp
from jax import lax
from jax.experimental import pallas as pl
from jax.experimental.pallas import tpu as pltpu
from jax.sharding import PartitionSpec as P

F32 = jnp.float32
BF16 = jnp.bfloat16

C2, C1 = 384, 192
GRID_ROWS, GRID_COLS = 48, 256
RC, CC = 6, 16
RF, CF = 12, 32
HC, HF = 5, 4
EC, EF = RC + 2 * HC, RF + 2 * HF
PC = 32
QC, QF = 24, 40
PAD = 8
WF = 256
ROW_BUF, COL_BUF = 160, 144
TAPS = 9
KC = TAPS * C2 + 128

VMEM = pl.BlockSpec(memory_space=pltpu.VMEM)
SMEM = pl.BlockSpec(memory_space=pltpu.SMEM)
ANY = pl.BlockSpec(memory_space=pl.ANY)
HBM = pl.BlockSpec(memory_space=pltpu.HBM)


def dot(a, b):
    return jnp.dot(a, b, preferred_element_type=F32)


def dot_t(a, b):
    return lax.dot_general(a, b, (((1,), (1,)), ((), ())), preferred_element_type=F32)


def sigmoid(x):
    return 0.5 * jnp.tanh(0.5 * x) + 0.5


def iota(shape, dim):
    return lax.broadcasted_iota(jnp.int32, shape, dim)


def tiles_get(ref, rows):
    return jnp.concatenate([ref[t, rows, :] for t in range(ref.shape[0])], 1)


def pack_pair(a, b):
    return jnp.concatenate([a[:, 128:], b[:, 128:], a[:, :128] + pltpu.roll(b[:, :128], 64, 1)], 1)


def unpack_pair(both):
    mixed = both[:, 256:384]
    upper = iota(mixed.shape, 1) >= 64
    a = jnp.where(upper, mixed, 0.0)
    b = jnp.where(upper, pltpu.roll(mixed, 64, 1), 0.0)
    return jnp.concatenate([a, both[:, :128]], 1), jnp.concatenate([b, both[:, 128:256]], 1)


def tiles_put(ref, rows, value):
    lanes = ref.shape[0] * 128
    if value.shape[1] < lanes:
        value = jnp.concatenate([value, jnp.zeros((value.shape[0], lanes - value.shape[1]), F32)], 1)
    for t in range(ref.shape[0]):
        ref[t, rows, :] = value[:, 128 * t : 128 * t + 128]


def indicator(cond):
    return jnp.where(cond, 1.0, 0.0).astype(BF16)


def start_kernel(
    place,
    frames_hbm,
    noise_hbm,
    context2_hbm,
    context1_hbm,
    cand_hbm,
    gates_hbm,
    hc_out,
    hf_out,
    noise_out,
    even_out,
    odd_out,
    cand_out,
    gates_out,
    frames,
    noise,
    context2,
    context1,
    picks,
    swaps,
    spreads,
    buf,
    sem,
):
    moves = [
        pltpu.make_async_copy(src, dst, sem.at[i])
        for i, (src, dst) in enumerate(
            (
                (frames_hbm, frames),
                (context2_hbm, context2),
                (context1_hbm, context1.at[pl.ds(WF - C1, C1), :]),
                (noise_hbm, noise),
            )
        )
    ]
    weights = [
        pltpu.make_async_copy(
            cand_hbm.at[pl.ds(2 * C2 * t + C2, C2), :], cand_out.at[pl.ds(C2 * t, C2), :], sem.at[4 + t]
        )
        for t in range(TAPS)
    ]
    weights.append(pltpu.make_async_copy(gates_hbm, gates_out, sem.at[4 + TAPS]))
    for copy in moves + weights:
        copy.start()

    def pick(shift, parity):
        row, col = iota((128, 256), 0), iota((128, 256), 1)
        count = 256 >> shift
        j = 2 * (row >> (8 - shift)) + parity
        return indicator(col == ((row & (count - 1)) << shift) + j)

    context1[0 : WF - C1, :] = jnp.zeros((WF - C1, 256), BF16)
    for shift in (4, 3):
        for parity in range(2):
            picks[4 - shift, parity] = pick(shift, parity)
    row, col = iota((256, 256), 0), iota((256, 256), 1)
    swaps[...] = indicator(col == ((row & 15) << 4) + (row >> 4))
    row, col = iota((512, 256), 0), iota((512, 256), 1)
    source = (((row >> 4) & 3) << 6) + ((row & 7) << 3) + (row >> 6)
    for q in range(2):
        spreads[q] = indicator((col == source) & (((row >> 3) & 1) == q))
    moves[0].wait()
    zeros = jnp.zeros((64, 256), BF16)
    even, odd = [], []
    for r in range(RC):
        band = frames[:, 16 * r : 16 * r + 16, :].reshape(64, 256)
        even += [band, zeros]
        odd += [zeros, band]
    even, odd = jnp.concatenate(even, 0), jnp.concatenate(odd, 0)

    def turned(shift):
        both = dot_t(picks[4 - shift, 0], even) + dot_t(picks[4 - shift, 1], odd)
        return both.astype(BF16)

    deep = turned(3)
    left = jnp.concatenate(
        [
            jnp.concatenate([deep[32 * j : 32 * j + 32, 128 * r : 128 * r + 128] for r in range(RC)], 0)
            for j in range(4)
        ],
        1,
    )
    moves[2].wait()
    for q in range(2):
        weight = dot_t(spreads[q], context1[...]).astype(BF16)
        state1 = jnp.tanh(dot(left, weight)).astype(BF16)
        for r in range(RC):
            hf_out[2 * r + q] = state1[CF * r : CF * r + CF]

    deep = turned(4)
    left = jnp.concatenate(
        [
            jnp.concatenate([deep[16 * j : 16 * j + 16, 128 * r : 128 * r + 128] for r in range(RC)], 0)
            for j in range(8)
        ],
        1,
    )
    moves[1].wait()
    swap = swaps[...]
    moved = [dot(swap, context2[256 * f : 256 * f + 256, :]).astype(BF16) for f in range(4)]
    weight = jnp.concatenate([moved[f][16 * j : 16 * j + 16] for j in range(16) for f in range(4)], 0)
    state2 = jnp.tanh(dot(left, weight))
    hc_out[...] = state2.astype(BF16).reshape(RC, CC, C2)

    moves[3].wait()
    diagonal = indicator(iota((16, 16), 0) == iota((16, 16), 1))
    turned_noise = dot_t(diagonal, noise[...].reshape(RC * 8, CC))
    turned_noise = jnp.concatenate([turned_noise, jnp.zeros((16, 128 - 8 * RC), F32)], 1)
    noise_out[...] = turned_noise.astype(BF16)
    low_noise = pltpu.roll(turned_noise, 128 - 8 * (RC - HC), 1)

    up_first = (place[0] & 1) == 1
    for target, up in ((even_out, up_first), (odd_out, jnp.logical_not(up_first))):
        c_top = state2[: HC * CC]
        c_low = state2[(RC - HC) * CC :]
        buf[0:80, :] = jnp.where(up, c_top, c_low)
        top = [hf_out[r : r + 2].reshape(64, WF).astype(F32) for r in (0, 2)]
        low = [hf_out[r : r + 2].reshape(64, WF).astype(F32) for r in (RF - HF, RF - HF + 2)]
        buf[80:144, :] = jnp.where(up, pack_pair(*top), pack_pair(*low))
        buf[144:160, :] = jnp.zeros((16, C2), F32)
        buf[144:160, 0:128] = jnp.where(up, turned_noise, low_noise)
        target[...] = buf[...].astype(BF16)
    for copy in weights:
        copy.wait()


def column_kernel(
    place, hc, hf, noise, even_in, odd_in, after, ec_out, ef_out, en_out, even_out, odd_out, sc, sf, sn, buf
):
    up_first = (place[0] & 1) == 1
    above = jnp.where(up_first, even_in[...].astype(F32), odd_in[...].astype(F32))
    below = jnp.where(up_first, odd_in[...].astype(F32), even_in[...].astype(F32))
    tiles_put(sc, pl.ds(0, 80), above[0:80])
    tiles_put(sc, pl.ds(80, 96), hc[...].reshape(RC * CC, C2).astype(F32))
    tiles_put(sc, pl.ds(176, 80), below[0:80])
    for half, strip in enumerate(unpack_pair(above[80:144])):
        tiles_put(sf, pl.ds(64 * half, 64), strip)
    for half, strip in enumerate(unpack_pair(below[80:144])):
        tiles_put(sf, pl.ds(512 + 64 * half, 64), strip)
    tiles_put(sf, pl.ds(128, 384), hf[...].reshape(RF * CF, WF).astype(F32))
    tiles_put(sf, pl.ds(640, 128), jnp.zeros((128, WF), F32))
    sn[...] = jnp.zeros(sn.shape, F32)
    for h in range(HC):
        sn[16 * h : 16 * h + 16, 0:8] = above[144:160, 8 * h : 8 * h + 8]
        sn[16 * (HC + RC + h) : 16 * (HC + RC + h) + 16, 0:8] = below[144:160, 8 * h : 8 * h + 8]
    for h in range(RC):
        sn[16 * (HC + h) : 16 * (HC + h) + 16, 0:8] = noise[:, 8 * h : 8 * h + 8].astype(F32)

    ec_out[...] = tiles_get(sc, pl.ds(0, EC * CC)).astype(BF16).reshape(EC, CC, C2)
    ef_out[...] = tiles_get(sf, pl.ds(0, EF * CF)).astype(BF16).reshape(EF, CF, WF)
    en_out[...] = sn[...].astype(BF16).reshape(EC, CC, 128)

    left_first = (place[1] & 1) == 1
    for target, left in ((even_out, left_first), (odd_out, jnp.logical_not(left_first))):
        c_from = jnp.where(left, 0, CC - HC)
        f_from = jnp.where(left, 0, CF - HF)
        buf[128:144, :] = jnp.zeros((16, C2), F32)
        for k in range(HC):
            buf[16 * k : 16 * k + 16, :] = tiles_get(sc, pl.ds(c_from + k, 16, stride=CC))
            strip = sn[pl.ds(c_from + k, 16, stride=CC), :]
            buf[128:144, 8 * k : 8 * k + 8] = strip[:, 0:8]
        for k in range(2):
            strips = [tiles_get(sf, pl.ds(f_from + i, 24, stride=CF)) for i in (k, k + 2)]
            buf[80 + 24 * k : 104 + 24 * k, :] = pack_pair(*strips)
        target[...] = buf[...].astype(BF16)


def coarse_weights_kernel(
    proj_hbm, gates_hbm, cand_hbm, wg_out, wc_out, token, proj, gates, cand, acc_g, acc_c, sem
):
    count = [0]

    def move(src, dst):
        copy = pltpu.make_async_copy(src, dst, sem.at[count[0]])
        count[0] += 1
        copy.start()
        return copy

    first = move(proj_hbm, proj)
    inputs, states = [], []
    for hbm, held in ((gates_hbm, gates), (cand_hbm, cand)):
        inputs.append([move(hbm.at[pl.ds(2 * C2 * t, C2), :], held.at[t]) for t in range(TAPS)])
    for t in range(TAPS):
        states.append(move(gates_hbm.at[pl.ds(2 * C2 * t + C2, C2), :], wg_out.at[pl.ds(C2 * t, C2), :]))
    acc_g[...] = jnp.zeros(acc_g.shape, F32)
    acc_c[...] = jnp.zeros(acc_c.shape, F32)
    first.wait()
    token[...] = jnp.zeros(token.shape, F32)
    wide = jnp.concatenate([proj[...].astype(F32), jnp.zeros((8, C2), F32)], 0).astype(BF16)
    for copies, held, acc in ((inputs[0], gates, acc_g), (inputs[1], cand, acc_c)):
        for t in range(TAPS):
            copies[t].wait()
            acc[8 * t : 8 * t + 8, :] = dot(wide, held[t])[0:8]
    wg_out[TAPS * C2 :, :] = acc_g[...].astype(BF16)
    wc_out[...] = acc_c[...].astype(BF16)
    for copy in states:
        copy.wait()


def fine_weights_kernel(
    after, gates, cand_hbm, up_hbm, head_hbm, wr_out, wu_out, wv_out, wc_out, up_out, head_out, up, head, sem
):
    moves = [
        pltpu.make_async_copy(src, dst, sem.at[i])
        for i, (src, dst) in enumerate(
            (
                (up_hbm, up),
                (head_hbm, head),
                (cand_hbm, wc_out.at[pl.ds(WF - C1, C1), :]),
            )
        )
    ]
    for copy in moves:
        copy.start()
    wc_out[0 : WF - C1, :] = jnp.zeros((WF - C1, 18 * C1), BF16)
    moves[1].wait()
    row, col = iota((1024, 64), 0), iota((1024, 64), 1)
    spread = indicator(col == ((row >> 7) << 3) + (row & 7))
    wide = jnp.concatenate([jnp.zeros((64, WF - C1), F32), head[...].astype(F32)], 1).astype(BF16)
    head_out[...] = dot(spread, wide).astype(BF16)
    moves[0].wait()
    wide = up[...].astype(F32)
    zeros = jnp.zeros((C2, 256 - C1), F32)
    for i in range(4):
        part = jnp.concatenate([wide[:, C1 * i : C1 * i + C1], zeros], 1)
        up_out[:, 256 * i : 256 * i + 256] = part.astype(BF16)
    for t in range(TAPS):
        rows = slice(2 * C1 * t, 2 * C1 * t + 2 * C1)
        part = gates[rows, 0:256].astype(F32)
        wr_out[rows, :] = jnp.concatenate([part[:, C1:256], part[:, :C1]], 1).astype(BF16)
        target, lane = (wv_out, 0) if t % 3 == 1 else (wu_out, 64 * (t % 3))
        target[2 * C1 * (t // 3) : 2 * C1 * (t // 3) + 2 * C1, lane : lane + 128] = gates[rows, 256:384]
    moves[2].wait()


def main_kernel(
    place,
    ec,
    ef,
    en,
    odd_in,
    even_in,
    wg2,
    wc2,
    fold2,
    wr1,
    wu1,
    wv1,
    wc1,
    wup,
    whead,
    out,
    first_h,
    sn,
    patch,
    reset_h,
    next_h,
    gate_u,
    fine_x,
    fine_h,
    fine_reset,
    fine_u,
    side_u,
    even_c,
    odd_c,
    even_f,
    odd_f,
    last_f,
):
    row0, col0 = place[0], place[1]
    left_first = (col0 & 1) == 1
    left = jnp.where(left_first, even_in[...].astype(F32), odd_in[...].astype(F32))
    right = jnp.where(left_first, odd_in[...].astype(F32), even_in[...].astype(F32))

    for ref, pitch, rows in (
        (reset_h, QC, EC), (next_h, QC, EC), (fine_x, QF, EF), (fine_h, QF, EF), (fine_reset, QF, EF)
    ):
        for t in range(ref.shape[0]):
            ref[t, 0 : PAD + 2 * pitch, :] = jnp.zeros((PAD + 2 * pitch, 128), F32)
            ref[t, PAD + (rows - 2) * pitch :, :] = jnp.zeros((2 * pitch + 8, 128), F32)
    sn[...] = jnp.zeros(sn.shape, F32)
    for h in range(EC):
        tiles_put(first_h, pl.ds(PC * h + 8, CC), ec[h].astype(F32))
        sn[PC * h + 8 : PC * h + 24, :] = en[h].astype(F32)
    for k in range(HC):
        for side, at in ((left, 8 - HC + k), (right, 8 + CC + k)):
            tiles_put(first_h, pl.ds(at, EC, stride=PC), side[16 * k : 16 * k + 16])
            strip = jnp.concatenate([side[128:144, 8 * k : 8 * k + 8], jnp.zeros((16, 120), F32)], 1)
            sn[pl.ds(at, EC, stride=PC), :] = strip
    for h in range(EF):
        tiles_put(fine_h, pl.ds(PAD + QF * h + HF, CF), ef[h].astype(F32))
    for side, col in ((left, 0), (right, HF + CF)):
        for k in range(2):
            for i, strip in enumerate(unpack_pair(side[80 + 24 * k : 80 + 24 * k + EF])):
                tiles_put(fine_h, pl.ds(PAD + col + k + 2 * i, EF, stride=QF), strip)

    noise = sn[...].reshape(EC, PC, 128)
    total = None
    for dx in range(3):
        part = None
        for dy in range(3):
            moved = noise[dy : dy + EC - 2]
            if dy or dx:
                moved = pltpu.roll(moved, 8 * (3 * dy + dx), 2)
            part = moved if part is None else part + moved
        part = part[:, 3 + dx : 3 + dx + QC, :]
        total = part if total is None else total + part
    patch[...] = total.reshape((EC - 2) * QC, 128)

    def fill(even, odd, pitch, lane, first, last, window):
        for dx in range(3):
            for ref, start in ((even, first + first % 2), (odd, first + 1 - first % 2)):
                rows = last - first - 2 * (start != first)
                at = (start // 2) * 2 * pitch
                ref[dx, at : at + rows * pitch, lane : lane + 128] = window(start, rows, dx - 1).astype(BF16)

    def taps(even, odd, pitch, first, rows):
        parts = []
        for dy in range(3):
            start = first - 1 + dy
            ref = odd if start % 2 else even
            at = (start // 2) * 2 * pitch
            parts += [ref[dx, at : at + rows * pitch, :] for dx in range(3)]
        return parts

    def flat(ref, t, pitch):
        return lambda start, rows, shift: ref[t, pl.ds(PAD + start * pitch + shift, rows * pitch), :]

    def cells(ref, t, pitch, first, rows):
        return ref[t, pl.ds(PAD + first * pitch, rows * pitch), :]

    def valid(first, rows, pitch, row_own, col_own, scale):
        at = iota((rows, pitch, 128), 0) + (row_own * scale + first)
        col = iota((rows, pitch, 128), 1) + (col_own * scale)
        good = (at >= 0) & (at < GRID_ROWS * scale) & (col >= 0) & (col < GRID_COLS * scale)
        return good.reshape(rows * pitch, 128)

    def own_first(t, start, rows, shift):
        return jnp.concatenate(
            [first_h[t, pl.ds(PC * h + 4 + shift, QC), :] for h in range(start, start + rows)], 0
        )

    def coarse_left(first, rows):
        near = patch[QC * (first - 1) : QC * (first - 1 + rows), :].astype(BF16)
        return jnp.concatenate(taps(even_c, odd_c, QC, first, rows) + [near], 1)

    def coarse_ready(step):
        first, rows = 1 + 2 * step, 14 - 4 * step
        for t in range(3):
            if step == 0:
                window = functools.partial(own_first, t)
            else:
                window = flat(next_h, t, QC)
            fill(even_c, odd_c, QC, 128 * t, first - 1, first + rows + 1, window)

    def coarse_gates(step):
        first, rows = 1 + 2 * step, 14 - 4 * step
        operand = coarse_left(first, rows)
        gates = dot(operand, wg2[:, 0:512])
        for t in range(3):
            old = own_first(t, first, rows, 0) if step == 0 else cells(next_h, t, QC, first, rows)
            reset_h[t, pl.ds(PAD + QC * first, QC * rows), :] = sigmoid(gates[:, 128 * t : 128 * t + 128]) * old
        gate_u[0, pl.ds(PAD + QC * first, QC * rows), :] = sigmoid(gates[:, 384:512])
        gates = dot(coarse_left(first + 1, rows - 2), wg2[:, 512:768])
        for t in (1, 2):
            at = pl.ds(PAD + QC * (first + 1), QC * (rows - 2))
            gate_u[t, at, :] = sigmoid(gates[:, 128 * t - 128 : 128 * t])

    def coarse_cand(step):
        first, rows = 2 + 2 * step, 12 - 4 * step
        for t in range(3):
            fill(even_c, odd_c, QC, 128 * t, first - 1, first + rows + 1, flat(reset_h, t, QC))
        operand = coarse_left(first, rows)
        good = valid(first, rows, QC, row0 * RC - HC, col0 * CC - 4, 1)
        for lanes, here in ((slice(0, 256), (0, 1)), (slice(256, 384), (2,))):
            cand = jnp.tanh(dot(operand, jnp.concatenate([wc2[:, lanes], fold2[:, lanes]], 0)))
            for i, t in enumerate(here):
                new = cand[:, 128 * i : 128 * i + 128]
                old = own_first(t, first, rows, 0) if step == 0 else cells(next_h, t, QC, first, rows)
                new = new + cells(gate_u, t, QC, first, rows) * (old - new)
                new = jnp.where(good, new, 0.0).astype(BF16).astype(F32)
                next_h[t, pl.ds(PAD + QC * first, QC * rows), :] = new

    def fine_input(step):
        first, rows = 3 + step, 10 - 2 * step
        state = jnp.concatenate(
            [
                jnp.concatenate(
                    [next_h[t, pl.ds(PAD + QC * h + 2, QC), :] for h in range(first, first + rows)], 0
                )
                for t in range(3)
            ],
            1,
        ).astype(BF16)
        value = dot(state, wup[...])
        for q in range(2):
            for p in range(2):
                lane = 256 * (2 * q + p)
                for r in range(rows):
                    at = PAD + (2 * (first + r) - 6 + q) * QF + p
                    tiles_put(fine_x, pl.ds(at, 20, stride=2), value[QC * r : QC * r + 20, lane : lane + 256])

    def fine_mixed(state, first, last):
        fill(even_f, odd_f, QF, 128, first, last, lambda *w: flat(fine_x, 1, QF)(*w) + flat(state, 0, QF)(*w))

    def fine_before(step):
        first, rows = 1 + 2 * step, 18 - 4 * step
        fill(even_f, odd_f, QF, 256, first - 1, first + rows + 1, flat(fine_h, 1, QF))

    def fine_ready(step):
        first, rows = 1 + 2 * step, 18 - 4 * step
        fill(even_f, odd_f, QF, 0, first - 1, first + rows + 1, flat(fine_x, 0, QF))
        fine_mixed(fine_h, first - 1, first + rows + 1)

    def fine_gates(step):
        first, rows = 1 + 2 * step, 18 - 4 * step
        gates = dot(jnp.concatenate(taps(even_f, odd_f, QF, first, rows), 1), wr1[...])
        at = pl.ds(PAD + QF * first, QF * rows)
        gate = sigmoid(gates[:, 0:128])
        fine_reset[0, at, :] = gate * fine_h[0, at, :]
        fine_u[0, at, :] = pltpu.roll(gate, 64, 1)
        fine_reset[1, at, :] = sigmoid(gates[:, 128:256]) * fine_h[1, at, :]
        middle = jnp.concatenate(taps(even_f, odd_f, QF, first + 1, rows - 2)[1::3], 1)
        count = QF * (rows - 2)
        sides = dot(middle, wu1[...])
        for i in range(2):
            side_u[i, PAD : PAD + count, :] = sides[:, 128 * i : 128 * i + 128]
        gate = dot(middle, wv1[...]) + side_u[0, pl.ds(PAD - 1, count), :] + side_u[1, pl.ds(PAD + 1, count), :]
        fine_u[1, pl.ds(PAD + QF * (first + 1), count), :] = sigmoid(gate)

    def fine_cand_ready():
        first, rows = 2, 16
        fine_mixed(fine_reset, first - 1, first + rows + 1)
        fill(even_f, odd_f, QF, 256, first - 1, first + rows + 1, flat(fine_reset, 1, QF))

    def fine_cand():
        first, rows = 2, 16
        operand = jnp.concatenate(taps(even_f, odd_f, QF, first, rows), 1)
        good = valid(first, rows, QF, row0 * RC - HC + 3, col0 * CC - 2, 2)
        cand = jnp.tanh(dot_t(operand, wc1[...]))
        at = pl.ds(PAD + QF * first, QF * rows)
        for t in range(2):
            new = cand[:, 128 * t : 128 * t + 128]
            new = new + fine_u[t, at, :] * (fine_h[t, at, :] - new)
            fine_h[t, at, :] = jnp.where(good, new, 0.0).astype(BF16).astype(F32)

    def own_fine(ref, t, shift=0, first=HF, rows=RF):
        return jnp.concatenate(
            [ref[t, pl.ds(PAD + QF * h + HF + shift, CF), :] for h in range(first, first + rows)], 0
        )

    def fine_last():
        first, rows = HF - 1, RF + 2
        for dx in range(3):
            x1 = own_fine(fine_x, 1, dx - 1, first, rows) + own_fine(fine_reset, 0, dx - 1, first, rows)
            last_f[dx, :, 0:128] = own_fine(fine_x, 0, dx - 1, first, rows).astype(BF16)
            last_f[dx, :, 128:256] = x1.astype(BF16)
            last_f[dx, :, 256:384] = own_fine(fine_reset, 1, dx - 1, first, rows).astype(BF16)
        parts = [last_f[dx, CF * dy : CF * (dy + RF), :] for dy in range(3) for dx in range(3)]
        cand = jnp.tanh(dot_t(jnp.concatenate(parts, 1), wc1[...]))
        state = []
        for t in range(2):
            new = cand[:, 128 * t : 128 * t + 128]
            state.append(new + own_fine(fine_u, t) * (own_fine(fine_h, t) - new))
        return jnp.concatenate(state, 1).astype(BF16)

    def emit(step, state):
        rows = RF
        shape = (2 * rows, 8, 128)
        lane, cell = iota(shape, 2), iota(shape, 1)
        low, mine = lane < 64, ((lane >> 3) & 7) == cell
        lines = []
        for r in range(0, 8, 2):
            pair = dot_t(state, whead[128 * r : 128 * r + 256, :])
            for i in range(2):
                value = pair[:, 128 * i : 128 * i + 128].reshape(2 * rows, 2, 8, 128)
                lines.append(jnp.where(mine, jnp.where(low, value[:, 0], value[:, 1]), 0.0))
        for d in (1, 2, 4):
            here = (cell & d) == 0
            folded = []
            for i in range(0, len(lines), 2):
                a, b = lines[i], lines[i + 1]
                folded.append(jnp.where(here, a, b) + pltpu.roll(jnp.where(here, b, a), d, 1))
            lines = folded
        final = lines[0].reshape(rows, 2, 8, 128)
        for t in range(2):
            out[step, :, 128 * t : 128 * t + 128] = final[:, t].reshape(8 * rows, 128)

    coarse_ready(0)
    coarse_gates(0)
    fine_before(0)
    coarse_cand(0)
    coarse_ready(1)
    fine_input(0)
    coarse_gates(1)
    fine_ready(0)
    fine_gates(0)
    fine_cand_ready()
    coarse_cand(1)
    fine_cand()
    fine_input(1)
    fine_before(1)
    fine_ready(1)
    fine_gates(1)
    emit(0, jnp.concatenate([own_fine(fine_h, 0), own_fine(fine_h, 1)], 1).astype(BF16))
    emit(1, fine_last())


def in_hbm(value):
    return pltpu.with_memory_space_constraint(value, pltpu.HBM)


def swapped(value, axis, odd):
    pairs = []
    for i in range(odd, lax.axis_size(axis) - 1, 2):
        pairs += [(i, i + 1), (i + 1, i)]
    return lax.ppermute(value, axis, pairs)


def call(kernel, out_shape, in_specs, scratch, limit, flops, bytes_accessed, **extra):
    return pl.pallas_call(
        kernel,
        out_shape=out_shape,
        in_specs=in_specs,
        out_specs=[VMEM] * len(out_shape),
        scratch_shapes=scratch,
        compiler_params=pltpu.CompilerParams(vmem_limit_bytes=limit),
        cost_estimate=pl.CostEstimate(flops=flops, bytes_accessed=bytes_accessed, transcendentals=0),
        **extra,
    )


def on_device(
    context_frames,
    latent_noise,
    latent_proj,
    coarse_context,
    fine_context,
    coarse_gates,
    coarse_candidate,
    fine_gates,
    fine_candidate,
    upsample_proj,
    head_proj,
):
    place = jnp.stack([lax.axis_index("row"), lax.axis_index("col")]).astype(jnp.int32)
    shape = jax.ShapeDtypeStruct
    row_buf, col_buf = shape((ROW_BUF, C2), BF16), shape((COL_BUF, C2), BF16)

    hc, hf, noise, even, odd, wc2, gates1 = call(
        start_kernel,
        [
            shape((RC, CC, C2), BF16),
            shape((RF, CF, WF), BF16),
            shape((16, 128), BF16),
            row_buf,
            row_buf,
            shape((TAPS * C2, C2), BF16),
            shape((18 * C1, 2 * C1), BF16),
        ],
        [SMEM] + [HBM] * 6,
        [
            pltpu.VMEM((4, 16 * RC, 16 * CC), BF16),
            pltpu.VMEM((RC, 8, CC), BF16),
            pltpu.VMEM((1024, C2), BF16),
            pltpu.VMEM((WF, 256), BF16),
            pltpu.VMEM((2, 2, 128, 256), BF16),
            pltpu.VMEM((256, 256), BF16),
            pltpu.VMEM((2, 512, 256), BF16),
            pltpu.VMEM((ROW_BUF, C2), F32),
            pltpu.SemaphoreType.DMA((5 + TAPS,)),
        ],
        16 << 20, 10**9, 8 << 20,
    )(
        place,
        in_hbm(context_frames),
        in_hbm(latent_noise.transpose(0, 2, 1)),
        in_hbm(coarse_context),
        in_hbm(fine_context.T),
        in_hbm(coarse_candidate),
        in_hbm(fine_gates),
    )

    odd = swapped(odd, "row", 1)
    even = swapped(even, "row", 0)

    wg2, fold2, token = call(
        coarse_weights_kernel,
        [shape((KC, 2 * C2), BF16), shape((128, C2), BF16), shape((8, 128), F32)],
        [HBM] * 3,
        [
            pltpu.VMEM((8, C2), BF16),
            pltpu.VMEM((TAPS, C2, 2 * C2), BF16),
            pltpu.VMEM((TAPS, C2, C2), BF16),
            pltpu.VMEM((128, 2 * C2), F32),
            pltpu.VMEM((128, C2), F32),
            pltpu.SemaphoreType.DMA((3 * TAPS + 1,)),
        ],
        16 << 20, 10**9, 24 << 20,
    )(in_hbm(latent_proj), in_hbm(coarse_gates), in_hbm(coarse_candidate))

    ec, ef, en, even, odd = call(
        column_kernel,
        [
            shape((EC, CC, C2), BF16),
            shape((EF, CF, WF), BF16),
            shape((EC, CC, 128), BF16),
            col_buf,
            col_buf,
        ],
        [SMEM] + [VMEM] * 5 + [ANY],
        [
            pltpu.VMEM((3, EC * CC, 128), F32),
            pltpu.VMEM((2, 24 * CF, 128), F32),
            pltpu.VMEM((EC * CC, 128), F32),
            pltpu.VMEM((COL_BUF, C2), F32),
        ],
        8 << 20, 10**6, 2 << 20,
    )(place, hc, hf, noise, even, odd, token)

    odd = swapped(odd, "col", 1)
    even = swapped(even, "col", 0)

    wr1, wu1, wv1, wc1, up, head = call(
        fine_weights_kernel,
        [
            shape((18 * C1, 256), BF16),
            shape((6 * C1, 256), BF16),
            shape((6 * C1, 128), BF16),
            shape((WF, 18 * C1), BF16),
            shape((C2, 1024), BF16),
            shape((1024, WF), BF16),
        ],
        [ANY, VMEM] + [HBM] * 3,
        [
            pltpu.VMEM((C2, 4 * C1), BF16),
            pltpu.VMEM((64, C1), BF16),
            pltpu.SemaphoreType.DMA((4,)),
        ],
        12 << 20, 10**8, 8 << 20,
    )(en, gates1, in_hbm(fine_candidate.T), in_hbm(upsample_proj), in_hbm(head_proj.T))

    (forecast,) = call(
        main_kernel,
        [shape((2, 96, 256), F32)],
        [SMEM] + [VMEM] * 14,
        [
            pltpu.VMEM((3, EC * PC, 128), F32),
            pltpu.VMEM((EC * PC, 128), F32),
            pltpu.VMEM(((EC - 2) * QC, 128), F32),
            pltpu.VMEM((3, PAD + EC * QC + 8, 128), F32),
            pltpu.VMEM((3, PAD + EC * QC + 8, 128), F32),
            pltpu.VMEM((3, PAD + EC * QC + 8, 128), F32),
            pltpu.VMEM((2, PAD + EF * QF + 8, 128), F32),
            pltpu.VMEM((2, PAD + EF * QF + 8, 128), F32),
            pltpu.VMEM((2, PAD + EF * QF + 8, 128), F32),
            pltpu.VMEM((2, PAD + EF * QF + 8, 128), F32),
            pltpu.VMEM((2, PAD + 16 * QF + 8, 128), F32),
            pltpu.VMEM((3, EC * QC, C2), BF16),
            pltpu.VMEM((3, EC * QC, C2), BF16),
            pltpu.VMEM((3, EF * QF, 2 * C1), BF16),
            pltpu.VMEM((3, EF * QF, 2 * C1), BF16),
            pltpu.VMEM((3, (RF + 2) * CF, 2 * C1), BF16),
        ],
        26 << 20, 9 * 10**9, 30 << 20,
    )(place, ec, ef, en, odd, even, wg2, wc2, fold2, wr1, wu1, wv1, wc1, up, head)
    return forecast


def solution(mesh):
    return jax.shard_map(
        on_device,
        mesh=mesh,
        in_specs=(
            P(None, "row", "col"),
            P("row", "col", None),
            P(),
            P(),
            P(),
            P(),
            P(),
            P(),
            P(),
            P(),
            P(),
        ),
        out_specs=P(None, "row", "col"),
        check_vma=False,
    )
```
